256 devices in a mesh: half: 4 (over z_lo, core), dev: 64 (over z_hi, x, y).
Axes of the slice: x: 4, y: 4, z: 8 (z_hi: 4, z_lo: 2; z = z_hi * 2 + z_lo), core: 2. Of those that a mesh axis runs over, the one named last changes fastest.
Arguments:
- potential: bfloat16 [1024, 1024], P('dev'), may hold values from 0 to 3
- tilt_ids: int32 [256, 2], P('half'), may hold values from -128 to 128
- beam_index: int32 [256], P('half'), may hold values from 0 to 15
- beam_table: float32 [16, 2], replicated, may hold values from -0.75 to 0.75
- positions: int32 [1024, 2], P('dev'), may hold values from 0 to 1023, as said below
Outputs:
- intensity: float32 [1024, 16, 1024], P('dev', None, 'half')
The draws below stay inside these ranges and needn't reach their ends.
Inputs may be any that keep to these rules, and one draw needn't show every extreme that they name: `positions`: position p has its row between (p // 16) * 16 and (p // 16) * 16 + 15, the rows of its tile; the second entry is its column.
All inputs are finite; a program needn't handle non-finite values.
Results may differ from the reference program's by a relative error of at most 0.0041.
Values may be sent and summed in bfloat16 or wider, within the bound.
No kernel may reach another device: no remote copies, remote signals or barrier semaphores. Data moves between devices by JAX's collectives and lax.ppermute only.
A program may use at most 128 MiB of HBM per device.

```python
import math
import jax
import jax.numpy as jnp
from jax import lax

N = 1024
LEVELS = 16
POS_TILE = 16
TILTS = 256
ROWS = 16
POSITIONS = 1024
N_DEV = 64


def draw_positions(key, part):
    key = jax.random.fold_in(key, 7)
    row_key, col_key = jax.random.split(key)
    tile_of = jnp.arange(POSITIONS, dtype=jnp.int32) // POS_TILE
    rows_drawn = tile_of * ROWS + jax.random.randint(row_key, (POSITIONS,), 0, ROWS, dtype=jnp.int32)
    cols_drawn = jax.random.randint(col_key, (POSITIONS,), 0, N, dtype=jnp.int32)
    rows_drawn = rows_drawn.at[0].set(0).at[POSITIONS - 1].set(N - 1)
    cols_drawn = cols_drawn.at[0].set(0).at[POSITIONS - 1].set(N - 1)
    return jnp.stack([rows_drawn, cols_drawn], axis=1)


def touch_ends(entries, rng, smallest, top_value):
    index_at = [jax.random.randint(jax.random.fold_in(rng, axis), (), 0, length) for axis, length in enumerate(entries.shape)]
    longest = entries.shape.index(max(entries.shape))
    next_to = index_at[:longest] + [(index_at[longest] + 1) % entries.shape[longest]] + index_at[longest + 1:]
    return entries.at[tuple(index_at)].set(smallest).at[tuple(next_to)].set(top_value)


def level_of(stream_key, shape, pieces, low, largest):
    def one(position, parts):
        steps = jax.random.uniform(jax.random.fold_in(jax.random.fold_in(stream_key, 6), position), (parts,), jnp.float32, low / len(pieces), largest / len(pieces))
        return jnp.repeat(jnp.exp(steps), shape[position] // parts).reshape((-1,) + (1,) * (len(shape) - position - 1))

    gain = one(*pieces[0])
    for cut in pieces[1:]:
        gain = gain * one(*cut)
    return gain


def gaussian(own_key, shape, spread, limit, kind=jnp.bfloat16):
    return jnp.clip(spread * jax.random.normal(own_key, shape, jnp.float32), -limit, limit).astype(kind)


def setup_inputs(seed: int = 0) -> dict:
    streams_of = jax.random.split(jax.random.key(seed), 6)
    potential = jnp.clip(3.0 * jax.random.uniform(streams_of[0], (N, N), jnp.float32) ** level_of(streams_of[0], (N, N), ((0, 64),), -0.2, 0.2), 0.0, 3.0).astype(jnp.bfloat16)
    tilt_ids = touch_ends(jax.random.randint(streams_of[1], (TILTS, 2), 0 - N // 8, N // 8 + 1), jax.random.fold_in(streams_of[1], 1), 0 - N // 8, (N // 8 + 1) - 1).astype(jnp.int32)
    beam_index = touch_ends(jax.random.randint(streams_of[2], (TILTS,), 0, LEVELS), jax.random.fold_in(streams_of[2], 1), 0, LEVELS - 1).astype(jnp.int32)
    beam_table = gaussian(streams_of[3], (LEVELS, 2), (2.0 / TILTS ** 0.5), 0.75, jnp.float32)
    positions = draw_positions(jax.random.fold_in(streams_of[5], 71), 0)
    return {"potential": potential, "tilt_ids": tilt_ids, "beam_index": beam_index, "beam_table": beam_table, "positions": positions}


two_pi = 2.0 * math.pi
propagation_rate = 0.6


def propagator():
    indices = jnp.arange(N, dtype=jnp.int32)
    signed = jnp.where(indices < N // 2, indices, indices - N)
    squared = signed[:, None] * signed[:, None] + signed[None, :] * signed[None, :]
    kept_mask = 9 * squared < N * N
    angle_field = -propagation_rate * squared.astype(jnp.float32) / N
    return jnp.where(kept_mask, jnp.cos(angle_field), 0.0), jnp.where(kept_mask, jnp.sin(angle_field), 0.0)


def rounded(values):
    narrow = values.astype(jnp.bfloat16)
    narrow = lax.optimization_barrier(narrow)
    return narrow.astype(jnp.float32)


def reference(potential, tilt_ids, beam_index, beam_table, positions):
    filter_re, filter_im = propagator()
    passband = lax.complex(filter_re, filter_im)
    coords = jnp.arange(N, dtype=jnp.int32)
    base_phase = potential.astype(jnp.float32)
    weights = beam_table[beam_index]
    winding = jnp.mod(positions[:, 0:1] * tilt_ids[None, :, 0] + positions[:, 1:2] * tilt_ids[None, :, 1], N)
    coef_angle = two_pi * winding.astype(jnp.float32) / N
    cosine = jnp.cos(coef_angle)
    sine_part = jnp.sin(coef_angle)
    coef_re = rounded(weights[None, :, 0] * cosine + weights[None, :, 1] * sine_part).reshape(N_DEV, POS_TILE, TILTS)
    coef_im = rounded(weights[None, :, 1] * cosine - weights[None, :, 0] * sine_part).reshape(N_DEV, POS_TILE, TILTS)
    group_size = math.gcd(TILTS, 16)
    blocks = TILTS // group_size

    def one_group(totals, group_index):
        first_tilt = (group_index * group_size).astype(jnp.int32)
        tilts_here = lax.dynamic_slice_in_dim(tilt_ids, first_tilt, group_size, 0)
        winding_field = jnp.mod(tilts_here[:, 0, None, None] * coords[None, :, None] + tilts_here[:, 1, None, None] * coords[None, None, :], N)
        phase_field = base_phase[None] + two_pi * winding_field.astype(jnp.float32) / N
        incident = lax.complex(jnp.cos(phase_field), jnp.sin(phase_field))
        exit_wave = jnp.fft.ifft2(jnp.fft.fft2(incident, axes=(1, 2)) * passband[None], axes=(1, 2))
        smat_re = rounded(jnp.real(exit_wave)).reshape(group_size, N_DEV, ROWS, N)
        smat_im = rounded(jnp.imag(exit_wave)).reshape(group_size, N_DEV, ROWS, N)
        part_re = lax.dynamic_slice_in_dim(coef_re, first_tilt, group_size, 2)
        part_im = lax.dynamic_slice_in_dim(coef_im, first_tilt, group_size, 2)
        total_re = totals[0] + jnp.einsum("tpg,gtry->tpry", part_re, smat_re) - jnp.einsum("tpg,gtry->tpry", part_im, smat_im)
        total_im = totals[1] + jnp.einsum("tpg,gtry->tpry", part_re, smat_im) + jnp.einsum("tpg,gtry->tpry", part_im, smat_re)
        return (total_re, total_im), None

    zeros_start = jnp.zeros((N_DEV, POS_TILE, ROWS, N), jnp.float32)
    totals, _ = lax.scan(one_group, (zeros_start, zeros_start), jnp.arange(blocks, dtype=jnp.int32))
    intensity = totals[0] * totals[0] + totals[1] * totals[1]
    return intensity.reshape(POSITIONS, ROWS, N)
```

```python
import functools
import math

import jax
import jax.numpy as jnp
import ml_dtypes
import numpy as np
from jax import lax
from jax.experimental import pallas as pl
from jax.experimental.pallas import tpu as pltpu
from jax.sharding import PartitionSpec as P

two_pi = 2.0 * math.pi
propagation_rate = 0.6

GRID = 1024
TILTS = 256
REACH = 128
BAND = 341
GROUP = 8
HALVES = 4
TILE = 16
WIDE = 24
PARTS = GROUP * HALVES
ROWS_IN = WIDE + 2 * REACH
HALF_COLS = GROUP * WIDE + 2 * REACH
KU = 768
BATCH = 16
BLOCK = 2 * BATCH * WIDE


def spread_of(count):
    return 2.0 ** np.mod(np.arange(count) * 0.6180339887498949, 1.0)


def angles(product):
    return np.mod(product, GRID).astype(np.float64) * (2.0 * np.pi / GRID)


def two_parts(table):
    high = table.astype(np.float32).astype(ml_dtypes.bfloat16)
    low = (table - high.astype(np.float64)).astype(np.float32).astype(ml_dtypes.bfloat16)
    return high, low


@functools.lru_cache(maxsize=None)
def column_table():
    angle = angles(np.arange(GRID)[:, None] * np.arange(HALF_COLS)[None, :])
    return np.concatenate([np.cos(angle), np.sin(angle)], 1).astype(np.float32)


@functools.lru_cache(maxsize=None)
def row_table():
    source, depth, inner = np.meshgrid(np.arange(16), np.arange(4), np.arange(16), indexing="ij")
    rows = ((depth * 16 + source) * 16 + inner).reshape(-1)
    angle = angles(rows[:, None] * (np.arange(GRID) - BAND - REACH)[None, :])
    table = np.concatenate([np.cos(angle), np.sin(angle)], 1)
    return two_parts(table / spread_of(TILE)[rows % TILE][:, None])


@functools.lru_cache(maxsize=None)
def back_row_table():
    index = np.arange(KU) - BAND
    result = []
    for group in range(8):
        rows = np.arange(GROUP * TILE) + group * GROUP * TILE
        angle = angles(index[:, None] * rows[None, :])
        angle = angle - (propagation_rate / GRID) * (index * index).astype(np.float64)[:, None]
        cosine, sine = np.cos(angle), np.sin(angle)
        result.append(np.concatenate([cosine, sine], 1))
    return np.stack(result).astype(np.float32).astype(ml_dtypes.bfloat16)


@functools.lru_cache(maxsize=None)
def back_column_table():
    index = np.arange(PARTS * WIDE) - BAND
    cols = np.arange(GRID)
    angle = angles(index[:, None] * cols[None, :])
    angle = angle - (propagation_rate / GRID) * (index * index).astype(np.float64)[:, None]
    scale = 1.0 / (GRID * GRID)
    cosine = (np.cos(angle) * scale).reshape(PARTS, WIDE, HALVES, GRID // HALVES)
    sine = (np.sin(angle) * scale).reshape(PARTS, WIDE, HALVES, GRID // HALVES)
    table = np.concatenate(
        [np.concatenate([cosine, sine], 3), np.concatenate([-sine, cosine], 3)], 1
    )
    table = table.reshape(PARTS * 2 * WIDE, HALVES, 2 * GRID // HALVES).transpose(1, 0, 2)
    return two_parts(table)


def field_kernel(
    shift_ref,
    start_ref,
    spread_ref,
    spec_re,
    spec_im,
    back_ref,
    coef_ref,
    level_ref,
    out_ref,
    mask,
    rows,
    field_re,
    field_im,
    sums_re,
    sums_im,
):
    first = start_ref[0]
    row_index = lax.broadcasted_iota(jnp.int32, (WIDE, KU), 0) + first
    lane_index = lax.broadcasted_iota(jnp.int32, (WIDE, KU), 1) - BAND
    inside = 9 * (row_index * row_index + lane_index * lane_index) < GRID * GRID
    inside = jnp.where(inside, 1.0, 0.0)
    mask[...] = jnp.concatenate([inside, inside], 0).astype(jnp.bfloat16)
    chunks = KU // 128

    def shifted(tilt, at):
        row_at = shift_ref[1, tilt]
        lane_at = shift_ref[0, tilt]
        spread = spread_ref[tilt]
        base = jnp.where(lane_at >= 128, 1, 0)
        rest = lane_at - 128 * base
        lanes = lax.broadcasted_iota(jnp.int32, (2 * WIDE, 128), 1)
        keep = lanes < 128 - rest
        turn = jnp.bitwise_and(128 - rest, 127)
        before = None
        for chunk in range(chunks + 1):
            window = jnp.concatenate(
                [ref[base + chunk, pl.ds(row_at, WIDE), :] for ref in (spec_re, spec_im)], 0
            )
            rolled = pltpu.roll((window * spread).astype(jnp.bfloat16), turn, 1)
            if chunk:
                lanes_at = (chunk - 1) * 128
                rows[pl.ds(at, 2 * WIDE), lanes_at : lanes_at + 128] = (
                    jnp.where(keep, before, rolled) * mask[:, lanes_at : lanes_at + 128]
                )
            before = rolled

    def block(step, carry):
        for spot in range(BATCH):
            shifted(step * BATCH + spot, spot * 2 * WIDE)
        at = pl.multiple_of(step * BLOCK, BLOCK)
        result = jnp.dot(rows[...], back_ref[...], preferred_element_type=jnp.float32)
        field_re[pl.ds(at, BLOCK), :] = result[:, :128]
        field_im[pl.ds(at, BLOCK), :] = result[:, 128:]
        return carry

    lax.fori_loop(0, TILTS // BATCH, block, 0)

    count = GROUP * TILE
    for col in range(WIDE):
        values = jnp.concatenate(
            [
                jnp.concatenate(
                    [ref[pl.ds(col + WIDE * part, TILTS, stride=2 * WIDE), :] for part in range(2)], 0
                )
                * level_ref[...]
                for ref in (field_re, field_im)
            ],
            1,
        )
        high = values.astype(jnp.bfloat16)
        low = (values - high.astype(jnp.float32)).astype(jnp.bfloat16)
        mixed = jnp.dot(coef_ref[...], high, preferred_element_type=jnp.float32)
        mixed = mixed + jnp.dot(coef_ref[...], low, preferred_element_type=jnp.float32)
        sums_re[pl.ds(col, count, stride=WIDE), :] = mixed[:count, :count] - mixed[count:, count:]
        sums_im[pl.ds(col, count, stride=WIDE), :] = mixed[count:, :count] + mixed[:count, count:]

    block_of = lax.broadcasted_iota(jnp.int32, (WIDE, 128), 1) // TILE
    for tile in range(GROUP):
        for half in range(2):
            parts = []
            for ref in (sums_re, sums_im):
                total = jnp.zeros((WIDE, 128), jnp.float32)
                for spot in range(8):
                    at = (tile * TILE + half * 8 + spot) * WIDE
                    turned = ref[at : at + WIDE, :]
                    turn = ((spot - tile) * TILE) % 128
                    if turn:
                        turned = pltpu.roll(turned, turn, 1)
                    total = jnp.where(block_of == spot, turned, total)
                parts.append(total)
            out_ref[tile, :, half * 128 : (half + 1) * 128] = jnp.concatenate(parts, 0).astype(
                out_ref.dtype
            )


def field_sums(shifts, start, spec_re, spec_im, back, coef):
    vmem = pl.BlockSpec(memory_space=pltpu.VMEM)
    smem = pl.BlockSpec(memory_space=pltpu.SMEM)
    spread = spread_of(TILTS)
    level = np.tile(np.broadcast_to((1.0 / spread)[:, None], (TILTS, 128)), (2, 1))
    return pl.pallas_call(
        field_kernel,
        out_shape=jax.ShapeDtypeStruct((GROUP, 2 * WIDE, TILE * TILE), jnp.bfloat16),
        in_specs=[smem, smem, smem, vmem, vmem, vmem, vmem, vmem],
        out_specs=vmem,
        scratch_shapes=[
            pltpu.VMEM((2 * WIDE, KU), jnp.bfloat16),
            pltpu.VMEM((BLOCK, KU), jnp.bfloat16),
            pltpu.VMEM((TILTS * 2 * WIDE, 128), jnp.float32),
            pltpu.VMEM((TILTS * 2 * WIDE, 128), jnp.float32),
            pltpu.VMEM((GROUP * TILE * WIDE, 128), jnp.float32),
            pltpu.VMEM((GROUP * TILE * WIDE, 128), jnp.float32),
        ],
        compiler_params=pltpu.CompilerParams(vmem_limit_bytes=48 * 1024 * 1024),
    )(
        shifts,
        start,
        jnp.asarray(spread.astype(np.float32)),
        spec_re,
        spec_im,
        back,
        coef,
        jnp.asarray(level.astype(np.float32)),
    )


def mixing_table(tilt_list, beam_list, beam_table, positions):
    levels = beam_table.shape[0]
    selector = (beam_list[:, None] == jnp.arange(levels, dtype=jnp.int32)[None, :]).astype(
        jnp.float32
    )
    weights = jnp.dot(selector, beam_table, precision=lax.Precision.HIGHEST)
    winding = jnp.bitwise_and(
        positions[:, 0:1] * tilt_list[None, :, 0] + positions[:, 1:2] * tilt_list[None, :, 1],
        GRID - 1,
    )
    coef_angle = two_pi * winding.astype(jnp.float32) / GRID
    cosine = jnp.cos(coef_angle)
    sine_part = jnp.sin(coef_angle)
    coef_re = weights[None, :, 0] * cosine + weights[None, :, 1] * sine_part
    coef_im = weights[None, :, 1] * cosine - weights[None, :, 0] * sine_part
    return jnp.concatenate(
        [jnp.concatenate([coef_re, -coef_im], 1), jnp.concatenate([coef_im, coef_re], 1)], 0
    ).astype(jnp.bfloat16)


def groups(kind):
    flat = np.arange(64).reshape(4, 2, 2, 4)
    if kind == "depth":
        return flat.reshape(4, 16).T.tolist()
    if kind == "plane":
        return flat.reshape(4, 16).tolist()
    return flat.reshape(8, 8).tolist()


def local(potential, tilt_ids, beam_index, beam_table, positions):
    half = lax.axis_index("half")
    dev = lax.axis_index("dev")
    group, member = dev // GROUP, dev % GROUP

    tilt_info = lax.all_gather(
        jnp.concatenate([tilt_ids, beam_index[:, None]], 1), "half", axis=0, tiled=True
    )
    spots = lax.all_gather(
        positions, "dev", axis=0, tiled=True, axis_index_groups=groups("tiles")
    )
    coef = mixing_table(tilt_info[:, :2], tilt_info[:, 2], beam_table, spots)

    first_col = half * (GROUP * WIDE) - BAND - REACH
    turn = jnp.bitwise_and(first_col * jnp.arange(GRID, dtype=jnp.int32), GRID - 1)
    phase = potential.astype(jnp.float32) - (two_pi / GRID) * turn.astype(jnp.float32)[None, :]
    spread = jnp.asarray(spread_of(TILE).astype(np.float32))[:, None]
    wave = jnp.concatenate([jnp.cos(phase) * spread, jnp.sin(phase) * spread], 0)
    mixed = jnp.dot(wave, jnp.asarray(column_table()), precision=lax.Precision.HIGH)
    rows = potential.shape[0]
    cols_re = mixed[:rows, :HALF_COLS] + mixed[rows:, HALF_COLS:]
    cols_im = mixed[rows:, :HALF_COLS] - mixed[:rows, HALF_COLS:]
    piece = jnp.concatenate([cols_re, cols_im], 1).astype(jnp.bfloat16)

    piece = jnp.broadcast_to(piece[None], (4,) + piece.shape)
    piece = lax.all_to_all(
        piece, "dev", 0, 0, tiled=True, axis_index_groups=groups("depth")
    ).reshape(4 * rows, 2 * HALF_COLS)
    windows = jnp.stack(
        [
            jnp.concatenate(
                [
                    piece[:, WIDE * i : WIDE * i + ROWS_IN],
                    piece[:, HALF_COLS + WIDE * i : HALF_COLS + WIDE * i + ROWS_IN],
                ],
                1,
            )
            for i in range(GROUP)
        ]
    )
    windows = jnp.concatenate([windows, windows], 0)
    columns = lax.all_to_all(
        windows, "dev", 0, 0, tiled=True, axis_index_groups=groups("plane")
    ).reshape(GRID, 2 * ROWS_IN)

    high, low = row_table()
    dims = (((0,), (0,)), ((), ()))
    product = lax.dot_general(
        columns, jnp.asarray(high), dims, preferred_element_type=jnp.float32
    ) + lax.dot_general(columns, jnp.asarray(low), dims, preferred_element_type=jnp.float32)
    spec_re = product[:ROWS_IN, :GRID] + product[ROWS_IN:, GRID:]
    spec_im = product[ROWS_IN:, :GRID] - product[:ROWS_IN, GRID:]
    spec_re, spec_im = (
        x.reshape(ROWS_IN, GRID // 128, 128).transpose(1, 0, 2) for x in (spec_re, spec_im)
    )

    back = lax.dynamic_index_in_dim(jnp.asarray(back_row_table()), group, 0, keepdims=False)
    shifts = (REACH - tilt_info[:, :2]).T
    start = (WIDE * (half * GROUP + member) - BAND).reshape(1)
    sums = field_sums(shifts, start, spec_re, spec_im, back, coef)

    sums = lax.all_to_all(sums, "dev", 0, 0, tiled=True, axis_index_groups=groups("tiles"))
    sums = lax.all_gather(sums, "half", axis=0, tiled=True).reshape(PARTS * 2 * WIDE, TILE * TILE)

    high, low = (
        lax.dynamic_index_in_dim(jnp.asarray(t), half, 0, keepdims=False)
        for t in back_column_table()
    )
    probe = lax.dot_general(sums, high, dims, preferred_element_type=jnp.float32) + lax.dot_general(
        sums, low, dims, preferred_element_type=jnp.float32
    )
    share = GRID // HALVES
    real, imag = probe[:, :share], probe[:, share:]
    return (real * real + imag * imag).reshape(TILE, TILE, share)


def solution(mesh):
    return jax.shard_map(
        local,
        mesh=mesh,
        in_specs=(P("dev", None), P("half", None), P("half"), P(), P("dev", None)),
        out_specs=P("dev", None, "half"),
        check_vma=False,
    )
```

```python
import functools
import math

import jax
import jax.numpy as jnp
import ml_dtypes
import numpy as np
from jax import lax
from jax.experimental import pallas as pl
from jax.experimental.pallas import tpu as pltpu
from jax.sharding import PartitionSpec as P

two_pi = 2.0 * math.pi
propagation_rate = 0.6

GRID = 1024
TILTS = 256
REACH = 128
BAND = 341
GROUP = 8
HALVES = 4
TILE = 16
WIDE = 24
PARTS = GROUP * HALVES
ROWS_IN = WIDE + 2 * REACH
HALF_COLS = GROUP * WIDE + 2 * REACH
KU = 768
BATCH = 16
BLOCK = 2 * BATCH * WIDE


def spread_of(count):
    return 2.0 ** np.mod(np.arange(count) * 0.6180339887498949, 1.0)


def angles(product):
    return np.mod(product, GRID).astype(np.float64) * (2.0 * np.pi / GRID)


def two_parts(table):
    high = table.astype(np.float32).astype(ml_dtypes.bfloat16)
    low = (table - high.astype(np.float64)).astype(np.float32).astype(ml_dtypes.bfloat16)
    return high, low


@functools.lru_cache(maxsize=None)
def column_table():
    angle = angles(np.arange(GRID)[:, None] * np.arange(HALF_COLS)[None, :])
    return np.concatenate([np.cos(angle), np.sin(angle)], 1).astype(np.float32)


@functools.lru_cache(maxsize=None)
def row_table():
    source, depth, inner = np.meshgrid(np.arange(16), np.arange(4), np.arange(16), indexing="ij")
    rows = ((depth * 16 + source) * 16 + inner).reshape(-1)
    angle = angles(rows[:, None] * (np.arange(GRID) - BAND - REACH)[None, :])
    table = np.stack([np.cos(angle), np.sin(angle)], 1).reshape(GRID, 2, GRID // 128, 128)
    table = table.transpose(0, 2, 1, 3).reshape(GRID, 2 * GRID)
    table = table / spread_of(TILE)[rows % TILE][:, None]
    return table.astype(np.float32).astype(ml_dtypes.bfloat16)


@functools.lru_cache(maxsize=None)
def back_row_table():
    index = np.arange(KU) - BAND
    result = []
    for group in range(8):
        rows = np.arange(GROUP * TILE) + group * GROUP * TILE
        angle = angles(index[:, None] * rows[None, :])
        angle = angle - (propagation_rate / GRID) * (index * index).astype(np.float64)[:, None]
        cosine, sine = np.cos(angle), np.sin(angle)
        result.append(np.concatenate([cosine, sine], 1))
    return np.stack(result).astype(np.float32).astype(ml_dtypes.bfloat16)


@functools.lru_cache(maxsize=None)
def back_column_table():
    index = np.arange(PARTS * WIDE) - BAND
    cols = np.arange(GRID)
    angle = angles(index[:, None] * cols[None, :])
    angle = angle - (propagation_rate / GRID) * (index * index).astype(np.float64)[:, None]
    scale = 1.0 / (GRID * GRID)
    cosine = (np.cos(angle) * scale).reshape(PARTS, WIDE, HALVES, GRID // HALVES)
    sine = (np.sin(angle) * scale).reshape(PARTS, WIDE, HALVES, GRID // HALVES)
    table = np.concatenate(
        [np.concatenate([cosine, sine], 3), np.concatenate([-sine, cosine], 3)], 1
    )
    table = table.reshape(PARTS * 2 * WIDE, HALVES, 2 * GRID // HALVES).transpose(1, 0, 2)
    return two_parts(table)


def window_kernel(piece_ref, out_ref):
    for member in range(GROUP):
        at = WIDE * member
        for part in range(2):
            from_at = part * HALF_COLS + at
            window = piece_ref[:, from_at : from_at + ROWS_IN]
            for copy in range(2):
                out_ref[member + copy * GROUP, :, part * ROWS_IN : (part + 1) * ROWS_IN] = window


def windows_of(piece):
    vmem = pl.BlockSpec(memory_space=pltpu.VMEM)
    return pl.pallas_call(
        window_kernel,
        out_shape=jax.ShapeDtypeStruct((2 * GROUP, piece.shape[0], 2 * ROWS_IN), piece.dtype),
        in_specs=[vmem],
        out_specs=vmem,
    )(piece)


def field_kernel(
    shift_ref,
    start_ref,
    spread_ref,
    columns_ref,
    table_ref,
    back_ref,
    coef_ref,
    level_ref,
    out_ref,
    turned_ref,
    spec_re,
    spec_im,
    mask,
    rows_a,
    rows_b,
    field_re,
    field_im,
    sums_re,
    sums_im,
):
    turned_ref[...] = columns_ref[...].T
    for chunk in range(GRID // 128):
        both = jnp.dot(
            turned_ref[...],
            table_ref[:, chunk * 256 : (chunk + 1) * 256],
            preferred_element_type=jnp.float32,
        )
        spec_re[chunk] = both[:ROWS_IN, :128] + both[ROWS_IN:, 128:]
        spec_im[chunk] = both[ROWS_IN:, :128] - both[:ROWS_IN, 128:]

    first = start_ref[0]
    row_index = lax.broadcasted_iota(jnp.int32, (WIDE, KU), 0) + first
    lane_index = lax.broadcasted_iota(jnp.int32, (WIDE, KU), 1) - BAND
    inside = 9 * (row_index * row_index + lane_index * lane_index) < GRID * GRID
    inside = jnp.where(inside, 1.0, 0.0)
    mask[...] = jnp.concatenate([inside, inside], 0).astype(jnp.bfloat16)
    chunks = KU // 128

    def shifted(tilt, rows, at):
        row_at = shift_ref[1, tilt]
        lane_at = shift_ref[0, tilt]
        spread = spread_ref[tilt]
        base = jnp.where(lane_at >= 128, 1, 0)
        rest = lane_at - 128 * base
        lanes = lax.broadcasted_iota(jnp.int32, (2 * WIDE, 128), 1)
        keep = lanes < 128 - rest
        turn = jnp.bitwise_and(128 - rest, 127)
        before = None
        for chunk in range(chunks + 1):
            window = jnp.concatenate(
                [ref[base + chunk, pl.ds(row_at, WIDE), :] for ref in (spec_re, spec_im)], 0
            )
            rolled = pltpu.roll((window * spread).astype(jnp.bfloat16), turn, 1)
            if chunk:
                lanes_at = (chunk - 1) * 128
                rows[at : at + 2 * WIDE, lanes_at : lanes_at + 128] = (
                    jnp.where(keep, before, rolled) * mask[:, lanes_at : lanes_at + 128]
                )
            before = rolled

    def fill(step, rows):
        for spot in range(BATCH):
            shifted(step * BATCH + spot, rows, spot * 2 * WIDE)

    def multiply(step, rows):
        at = pl.multiple_of(step * BLOCK, BLOCK)
        result = jnp.dot(rows[...], back_ref[...], preferred_element_type=jnp.float32)
        field_re[pl.ds(at, BLOCK), :] = result[:, :128]
        field_im[pl.ds(at, BLOCK), :] = result[:, 128:]

    steps = TILTS // BATCH
    fill(0, rows_a)

    def block(turn, carry):
        fill(2 * turn + 1, rows_b)
        multiply(2 * turn, rows_a)
        fill(jnp.minimum(2 * turn + 2, steps - 1), rows_a)
        multiply(2 * turn + 1, rows_b)
        return carry

    lax.fori_loop(0, steps // 2, block, 0)

    count = GROUP * TILE
    for col in range(WIDE):
        values = jnp.concatenate(
            [
                jnp.concatenate(
                    [ref[pl.ds(col + WIDE * part, TILTS, stride=2 * WIDE), :] for part in range(2)], 0
                )
                * level_ref[...]
                for ref in (field_re, field_im)
            ],
            1,
        )
        high = values.astype(jnp.bfloat16)
        low = (values - high.astype(jnp.float32)).astype(jnp.bfloat16)
        mixed = jnp.dot(coef_ref[...], high, preferred_element_type=jnp.float32)
        mixed = mixed + jnp.dot(coef_ref[...], low, preferred_element_type=jnp.float32)
        sums_re[pl.ds(col, count, stride=WIDE), :] = mixed[:count, :count] - mixed[count:, count:]
        sums_im[pl.ds(col, count, stride=WIDE), :] = mixed[count:, :count] + mixed[:count, count:]

    block_of = lax.broadcasted_iota(jnp.int32, (WIDE, 128), 1) // TILE
    for tile in range(GROUP):
        for half in range(2):
            parts = []
            for ref in (sums_re, sums_im):
                total = jnp.zeros((WIDE, 128), jnp.float32)
                for spot in range(8):
                    at = (tile * TILE + half * 8 + spot) * WIDE
                    turned = ref[at : at + WIDE, :]
                    turn = ((spot - tile) * TILE) % 128
                    if turn:
                        turned = pltpu.roll(turned, turn, 1)
                    total = jnp.where(block_of == spot, turned, total)
                parts.append(total)
            out_ref[tile, :, half * 128 : (half + 1) * 128] = jnp.concatenate(parts, 0).astype(
                out_ref.dtype
            )


def field_sums(shifts, start, columns, table, back, coef):
    vmem = pl.BlockSpec(memory_space=pltpu.VMEM)
    smem = pl.BlockSpec(memory_space=pltpu.SMEM)
    spread = spread_of(TILTS)
    level = np.tile(np.broadcast_to((1.0 / spread)[:, None], (TILTS, 128)), (2, 1))
    return pl.pallas_call(
        field_kernel,
        out_shape=jax.ShapeDtypeStruct((GROUP, 2 * WIDE, TILE * TILE), jnp.bfloat16),
        in_specs=[smem, smem, smem, vmem, vmem, vmem, vmem, vmem],
        out_specs=vmem,
        scratch_shapes=[
            pltpu.VMEM((2 * ROWS_IN, GRID), jnp.bfloat16),
            pltpu.VMEM((GRID // 128, ROWS_IN, 128), jnp.float32),
            pltpu.VMEM((GRID // 128, ROWS_IN, 128), jnp.float32),
            pltpu.VMEM((2 * WIDE, KU), jnp.bfloat16),
            pltpu.VMEM((BLOCK, KU), jnp.bfloat16),
            pltpu.VMEM((BLOCK, KU), jnp.bfloat16),
            pltpu.VMEM((TILTS * 2 * WIDE, 128), jnp.float32),
            pltpu.VMEM((TILTS * 2 * WIDE, 128), jnp.float32),
            pltpu.VMEM((GROUP * TILE * WIDE, 128), jnp.float32),
            pltpu.VMEM((GROUP * TILE * WIDE, 128), jnp.float32),
        ],
        compiler_params=pltpu.CompilerParams(vmem_limit_bytes=48 * 1024 * 1024),
    )(
        shifts,
        start,
        jnp.asarray(spread.astype(np.float32)),
        columns,
        table,
        back,
        coef,
        jnp.asarray(level.astype(np.float32)),
    )


def probe_kernel(sums_ref, high_ref, low_ref, out_ref):
    sums = sums_ref[...].T
    probe = jnp.dot(sums, high_ref[...], preferred_element_type=jnp.float32) + jnp.dot(
        sums, low_ref[...], preferred_element_type=jnp.float32
    )
    share = out_ref.shape[1]
    real, imag = probe[:, :share], probe[:, share:]
    out_ref[...] = real * real + imag * imag


def probe_intensity(sums, high, low):
    vmem = pl.BlockSpec(memory_space=pltpu.VMEM)
    return pl.pallas_call(
        probe_kernel,
        out_shape=jax.ShapeDtypeStruct((sums.shape[1], high.shape[1] // 2), jnp.float32),
        in_specs=[vmem] * 3,
        out_specs=vmem,
        compiler_params=pltpu.CompilerParams(vmem_limit_bytes=32 * 1024 * 1024),
    )(sums, high, low)


def mixing_table(tilt_list, beam_list, beam_table, positions):
    levels = beam_table.shape[0]
    selector = (beam_list[:, None] == jnp.arange(levels, dtype=jnp.int32)[None, :]).astype(
        jnp.float32
    )
    weights = jnp.dot(selector, beam_table, precision=lax.Precision.HIGHEST)
    winding = jnp.bitwise_and(
        positions[:, 0:1] * tilt_list[None, :, 0] + positions[:, 1:2] * tilt_list[None, :, 1],
        GRID - 1,
    )
    coef_angle = two_pi * winding.astype(jnp.float32) / GRID
    cosine = jnp.cos(coef_angle)
    sine_part = jnp.sin(coef_angle)
    coef_re = weights[None, :, 0] * cosine + weights[None, :, 1] * sine_part
    coef_im = weights[None, :, 1] * cosine - weights[None, :, 0] * sine_part
    return jnp.concatenate(
        [jnp.concatenate([coef_re, -coef_im], 1), jnp.concatenate([coef_im, coef_re], 1)], 0
    ).astype(jnp.bfloat16)


def doubled(block, axis, place, strides, size):
    for stride in strides:
        other = lax.ppermute(block, axis, [(i, i ^ stride) for i in range(size)])
        upper = jnp.bitwise_and(place, stride) != 0
        block = jnp.concatenate(
            [jnp.where(upper, other, block), jnp.where(upper, block, other)], 0
        )
    return block


def groups(kind):
    flat = np.arange(64).reshape(4, 2, 2, 4)
    if kind == "depth":
        return flat.reshape(4, 16).T.tolist()
    if kind == "plane":
        return flat.reshape(4, 16).tolist()
    return flat.reshape(8, 8).tolist()


def local(potential, tilt_ids, beam_index, beam_table, positions):
    half = lax.axis_index("half")
    dev = lax.axis_index("dev")
    group, member = dev // GROUP, dev % GROUP

    tilt_info = doubled(
        jnp.concatenate([tilt_ids, beam_index[:, None]], 1), "half", half, (1, 2), HALVES
    )
    spots = doubled(positions, "dev", dev, (1, 2, 4), 64)
    coef = mixing_table(tilt_info[:, :2], tilt_info[:, 2], beam_table, spots)

    first_col = half * (GROUP * WIDE) - BAND - REACH
    turn = jnp.bitwise_and(first_col * jnp.arange(GRID, dtype=jnp.int32), GRID - 1)
    phase = potential.astype(jnp.float32) - (two_pi / GRID) * turn.astype(jnp.float32)[None, :]
    spread = jnp.asarray(spread_of(TILE).astype(np.float32))[:, None]
    wave = jnp.concatenate([jnp.cos(phase) * spread, jnp.sin(phase) * spread], 0)
    mixed = jnp.dot(wave, jnp.asarray(column_table()), precision=lax.Precision.HIGH)
    rows = potential.shape[0]
    cols_re = mixed[:rows, :HALF_COLS] + mixed[rows:, HALF_COLS:]
    cols_im = mixed[rows:, :HALF_COLS] - mixed[:rows, HALF_COLS:]
    piece = jnp.concatenate([cols_re, cols_im], 1).astype(jnp.bfloat16)

    piece = jnp.broadcast_to(piece[None], (4,) + piece.shape)
    piece = lax.all_to_all(
        piece, "dev", 0, 0, tiled=True, axis_index_groups=groups("depth")
    ).reshape(4 * rows, 2 * HALF_COLS)
    columns = lax.all_to_all(
        windows_of(piece), "dev", 0, 0, tiled=True, axis_index_groups=groups("plane")
    ).reshape(GRID, 2 * ROWS_IN)

    back = lax.dynamic_index_in_dim(jnp.asarray(back_row_table()), group, 0, keepdims=False)
    shifts = (REACH - tilt_info[:, :2]).T
    start = (WIDE * (half * GROUP + member) - BAND).reshape(1)
    sums = field_sums(shifts, start, columns, jnp.asarray(row_table()), back, coef)

    sums = lax.all_to_all(sums, "dev", 0, 0, tiled=True, axis_index_groups=groups("tiles"))
    sums = lax.all_gather(sums, "half", axis=0, tiled=True).reshape(PARTS * 2 * WIDE, TILE * TILE)

    high, low = (
        lax.dynamic_index_in_dim(jnp.asarray(t), half, 0, keepdims=False)
        for t in back_column_table()
    )
    return probe_intensity(sums, high, low).reshape(TILE, TILE, GRID // HALVES)


def solution(mesh):
    return jax.shard_map(
        local,
        mesh=mesh,
        in_specs=(P("dev", None), P("half", None), P("half"), P(), P("dev", None)),
        out_specs=P("dev", None, "half"),
        check_vma=False,
    )
```

```python
import functools
import math

import jax
import jax.numpy as jnp
import ml_dtypes
import numpy as np
from jax import lax
from jax.experimental import pallas as pl
from jax.experimental.pallas import tpu as pltpu
from jax.sharding import PartitionSpec as P

two_pi = 2.0 * math.pi
propagation_rate = 0.6

GRID = 1024
TILTS = 256
REACH = 128
BAND = 341
GROUP = 8
HALVES = 4
TILE = 16
WIDE = 24
PARTS = GROUP * HALVES
ROWS_IN = 2 * WIDE + 2 * REACH
CHIP_COLS = GROUP * 2 * WIDE + 2 * REACH
NOTE = 4
LANES = 2 * ROWS_IN + NOTE
KU = 768
BATCH = 16
BLOCK = 2 * BATCH * WIDE


def spread_of(count):
    return 2.0 ** np.mod(np.arange(count) * 0.6180339887498949, 1.0)


def angles(product):
    return np.mod(product, GRID).astype(np.float64) * (2.0 * np.pi / GRID)


def two_parts(table):
    high = table.astype(np.float32).astype(ml_dtypes.bfloat16)
    low = (table - high.astype(np.float64)).astype(np.float32).astype(ml_dtypes.bfloat16)
    return high, low


@functools.lru_cache(maxsize=None)
def column_table():
    angle = angles(np.arange(GRID)[:, None] * np.arange(128)[None, :])
    return np.stack(two_parts(np.concatenate([np.cos(angle), np.sin(angle)], 1)))


@functools.lru_cache(maxsize=None)
def row_table():
    core, pair, source, depth, inner = np.meshgrid(
        np.arange(2), np.arange(2), np.arange(16), np.arange(4), np.arange(4), indexing="ij"
    )
    inner = 4 * inner + 2 * pair + core
    rows = ((depth * 16 + source) * TILE + inner).reshape(4, GRID // 4)
    angle = angles(rows[:, :, None] * (np.arange(GRID // 4) - BAND - REACH)[None, None, :])
    table = np.stack([np.cos(angle), np.sin(angle)], 2)
    table = table / spread_of(TILE)[rows % TILE][:, :, None, None]
    table = table.reshape(2, 2, GRID // 4, 2, 2, 128).transpose(0, 1, 2, 4, 3, 5)
    return table.reshape(2, 2, GRID // 4, 512).astype(np.float32).astype(ml_dtypes.bfloat16)


@functools.lru_cache(maxsize=None)
def back_row_table():
    index = np.arange(KU) - BAND
    result = []
    for group in range(8):
        rows = np.arange(GROUP * TILE) + group * GROUP * TILE
        angle = angles(index[:, None] * rows[None, :])
        angle = angle - (propagation_rate / GRID) * (index * index).astype(np.float64)[:, None]
        cosine, sine = np.cos(angle), np.sin(angle)
        result.append(np.concatenate([cosine, sine], 1))
    return np.stack(result).astype(np.float32).astype(ml_dtypes.bfloat16)


@functools.lru_cache(maxsize=None)
def back_column_table():
    chip, core, member = np.meshgrid(np.arange(2), np.arange(2), np.arange(GROUP), indexing="ij")
    part = (chip * 2 * GROUP + member * 2 + core).reshape(-1)
    index = (part[:, None] * WIDE + np.arange(WIDE)[None, :]).reshape(-1) - BAND
    cols = np.arange(GRID)
    angle = angles(index[:, None] * cols[None, :])
    angle = angle - (propagation_rate / GRID) * (index * index).astype(np.float64)[:, None]
    scale = 1.0 / (GRID * GRID)
    cosine = (np.cos(angle) * scale).reshape(PARTS, WIDE, HALVES, GRID // HALVES)
    sine = (np.sin(angle) * scale).reshape(PARTS, WIDE, HALVES, GRID // HALVES)
    table = np.concatenate(
        [np.concatenate([cosine, sine], 3), np.concatenate([-sine, cosine], 3)], 1
    )
    table = table.reshape(PARTS * 2 * WIDE, HALVES, 2 * GRID // HALVES).transpose(1, 0, 2)
    return two_parts(table)


def chosen(rows, cols, source):
    row = lax.broadcasted_iota(jnp.int32, (rows, cols), 0)
    col = lax.broadcasted_iota(jnp.int32, (rows, cols), 1)
    return jnp.where(col == source(row), 1.0, 0.0).astype(jnp.bfloat16)


def column_kernel(place_ref, field_ref, spread_ref, table_ref, out_ref, table, arrived):
    copy = pltpu.make_async_copy(table_ref, table, arrived)
    copy.start()
    first, core = place_ref[0], place_ref[1]
    rows = field_ref.shape[0] // 2
    pick = chosen(rows, 2 * rows, lambda row: 4 * (row % 4) + 2 * (row // 4) + core)
    field = jnp.dot(pick, field_ref[...], preferred_element_type=jnp.float32)
    spread = spread_ref[core][:, :1]
    column = lax.broadcasted_iota(jnp.int32, (rows, GRID), 1)
    waves = []
    for chunk in range(CHIP_COLS // 128):
        turn = jnp.bitwise_and((first + 128 * chunk) * column, GRID - 1)
        phase = field - (two_pi / GRID) * turn.astype(jnp.float32)
        waves += [jnp.cos(phase) * spread, jnp.sin(phase) * spread]
    wave = jnp.concatenate(waves, 0)
    high = wave.astype(jnp.bfloat16)
    low = (wave - high.astype(jnp.float32)).astype(jnp.bfloat16)
    count = wave.shape[0]
    copy.wait()
    both = jnp.dot(jnp.concatenate([high, low], 0), table[0], preferred_element_type=jnp.float32)
    mixed = both[:count] + both[count:]
    mixed = mixed + jnp.dot(high, table[1], preferred_element_type=jnp.float32)
    cols_re, cols_im = [], []
    for chunk in range(CHIP_COLS // 128):
        cosine = mixed[2 * rows * chunk : 2 * rows * chunk + rows]
        sine = mixed[2 * rows * chunk + rows : 2 * rows * (chunk + 1)]
        cols_re.append(cosine[:, :128] + sine[:, 128:])
        cols_im.append(sine[:, :128] - cosine[:, 128:])
    piece = jnp.concatenate(cols_re + cols_im, 1).astype(jnp.bfloat16)
    for copy in range(out_ref.shape[0]):
        out_ref[copy] = piece


def column_piece(place, potential):
    vmem = pl.BlockSpec(memory_space=pltpu.VMEM)
    smem = pl.BlockSpec(memory_space=pltpu.SMEM)
    table = column_table()
    rows = potential.shape[0]
    spread = spread_of(TILE).reshape(4, 2, 2).transpose(2, 1, 0).reshape(2, TILE // 2, 1)
    spread = np.broadcast_to(spread, (2, TILE // 2, 128)).astype(np.float32)
    return pl.pallas_call(
        column_kernel,
        out_shape=jax.ShapeDtypeStruct((4, rows // 2, 2 * CHIP_COLS), jnp.bfloat16),
        in_specs=[smem, vmem, vmem, pl.BlockSpec(memory_space=pl.ANY)],
        out_specs=vmem,
        scratch_shapes=[pltpu.VMEM(table.shape, jnp.bfloat16), pltpu.SemaphoreType.DMA],
        compiler_params=pltpu.CompilerParams(vmem_limit_bytes=16 * 1024 * 1024),
    )(place, potential, jnp.asarray(spread), jnp.asarray(table))


def window_kernel(piece_ref, note_ref, out_ref):
    rows = piece_ref.shape[0]
    pick = chosen(rows, rows, lambda row: 8 * ((row // 4) % 4) + 4 * (row // 16) + row % 4)
    piece = jnp.dot(pick, piece_ref[...], preferred_element_type=jnp.float32)
    note = note_ref[...]
    for member in range(GROUP):
        at = 2 * WIDE * member
        window = jnp.concatenate(
            [piece[:, part * CHIP_COLS + at : part * CHIP_COLS + at + ROWS_IN] for part in range(2)]
            + [note],
            1,
        ).astype(jnp.bfloat16)
        for copy in range(2):
            out_ref[member + copy * GROUP] = window


def windows_of(piece, note):
    vmem = pl.BlockSpec(memory_space=pltpu.VMEM)
    return pl.pallas_call(
        window_kernel,
        out_shape=jax.ShapeDtypeStruct((2 * GROUP, piece.shape[0], LANES), jnp.bfloat16),
        in_specs=[vmem, vmem],
        out_specs=vmem,
        compiler_params=pltpu.CompilerParams(vmem_limit_bytes=16 * 1024 * 1024),
    )(piece, note)


def field_kernel(
    shift_ref,
    start_ref,
    own_ref,
    mate_ref,
    table_ref,
    back_ref,
    coef_ref,
    out_ref,
    table,
    arrived,
    turned_ref,
    spec_re,
    spec_im,
    mask,
    rows_a,
    rows_b,
    field_re,
    field_im,
    sums_re,
    sums_im,
):
    copy = pltpu.make_async_copy(table_ref, table, arrived)
    copy.start()
    core = start_ref[1]
    for pair in range(2):
        for place, ref in ((core, own_ref), (1 - core, mate_ref)):
            block = ref[:, 16 * pair : 16 * pair + 16, :]
            block = block.reshape(GRID // 4, LANES)[:, : 2 * ROWS_IN]
            turned_ref[2 * pair + place] = block.T
    copy.wait()
    for part in range(2):
        lanes = slice(256 * part, 256 * (part + 1))
        each = []
        for remainder in range(4):
            both = jnp.dot(
                turned_ref[remainder],
                table[remainder % 2, remainder // 2, :, lanes],
                preferred_element_type=jnp.float32,
            )
            each.append(
                (
                    both[:ROWS_IN, :128] + both[ROWS_IN:, 128:],
                    both[ROWS_IN:, :128] - both[:ROWS_IN, 128:],
                )
            )
        (re0, im0), (re1, im1), (re2, im2), (re3, im3) = each
        even, even_less = (re0 + re2, im0 + im2), (re0 - re2, im0 - im2)
        odd, odd_less = (re1 + re3, im1 + im3), (im1 - im3, re3 - re1)
        for quarter, left, right, sign in (
            (0, even, odd, 1),
            (1, even_less, odd_less, 1),
            (2, even, odd, -1),
            (3, even_less, odd_less, -1),
        ):
            for ref, x, y in ((spec_re, left[0], right[0]), (spec_im, left[1], right[1])):
                ref[2 * quarter + part] = x + y if sign > 0 else x - y

    peak_row = start_ref[2]
    peak_at = jnp.clip(peak_row, 0, ROWS_IN - 1)
    peak_lane = BAND + REACH
    peak_re, peak_im = (
        ref[peak_lane // 128, pl.ds(peak_at, 1), :][:, peak_lane % 128 : peak_lane % 128 + 1]
        for ref in (spec_re, spec_im)
    )
    power = peak_re * peak_re + peak_im * peak_im
    held = jnp.logical_and(power > 1e-6, peak_row == peak_at)
    peak_re = jnp.where(held, peak_re, 1.0)
    peak_im = jnp.where(held, peak_im, 0.0)
    inverse = 1.0 / jnp.where(held, power, 1.0)
    scale_re, scale_im = peak_re * inverse, -peak_im * inverse
    for chunk in range(GRID // 128):
        value_re, value_im = spec_re[chunk], spec_im[chunk]
        spec_re[chunk] = value_re * scale_re - value_im * scale_im
        spec_im[chunk] = value_re * scale_im + value_im * scale_re

    first = start_ref[0]
    row_index = lax.broadcasted_iota(jnp.int32, (WIDE, KU), 0) + first
    lane_index = lax.broadcasted_iota(jnp.int32, (WIDE, KU), 1) - BAND
    inside = 9 * (row_index * row_index + lane_index * lane_index) < GRID * GRID
    inside = jnp.where(inside, 1.0, 0.0)
    mask[...] = jnp.concatenate([inside, inside], 0).astype(jnp.bfloat16)
    chunks = KU // 128

    def shifted(tilt, rows, at):
        row_at = shift_ref[1, tilt]
        lane_at = shift_ref[0, tilt]
        base = jnp.where(lane_at >= 128, 1, 0)
        rest = lane_at - 128 * base
        lanes = lax.broadcasted_iota(jnp.int32, (2 * WIDE, 128), 1)
        keep = lanes < 128 - rest
        turn = jnp.bitwise_and(128 - rest, 127)
        before = None
        for chunk in range(chunks + 1):
            window = jnp.concatenate(
                [ref[base + chunk, pl.ds(row_at, WIDE), :] for ref in (spec_re, spec_im)], 0
            )
            rolled = pltpu.roll(window.astype(jnp.bfloat16), turn, 1)
            if chunk:
                lanes_at = (chunk - 1) * 128
                rows[at : at + 2 * WIDE, lanes_at : lanes_at + 128] = (
                    jnp.where(keep, before, rolled) * mask[:, lanes_at : lanes_at + 128]
                )
            before = rolled

    def fill(step, rows):
        for spot in range(BATCH):
            shifted(step * BATCH + spot, rows, spot * 2 * WIDE)

    def multiply(step, rows):
        at = pl.multiple_of(step * BLOCK, BLOCK)
        result = jnp.dot(rows[...], back_ref[...], preferred_element_type=jnp.float32)
        field_re[pl.ds(at, BLOCK), :] = result[:, :128]
        field_im[pl.ds(at, BLOCK), :] = result[:, 128:]

    steps = TILTS // BATCH
    fill(0, rows_a)

    def block(turn, carry):
        fill(2 * turn + 1, rows_b)
        multiply(2 * turn, rows_a)
        fill(jnp.minimum(2 * turn + 2, steps - 1), rows_a)
        multiply(2 * turn + 1, rows_b)
        return carry

    lax.fori_loop(0, steps // 2, block, 0)

    count = GROUP * TILE
    for col in range(WIDE):
        values = jnp.concatenate(
            [
                jnp.concatenate(
                    [ref[pl.ds(col + WIDE * part, TILTS, stride=2 * WIDE), :] for part in range(2)], 0
                ).astype(jnp.bfloat16)
                for ref in (field_re, field_im)
            ],
            1,
        )
        mixed = jnp.dot(coef_ref[...], values, preferred_element_type=jnp.float32)
        sums_re[pl.ds(col, count, stride=WIDE), :] = mixed[:count, :count] - mixed[count:, count:]
        sums_im[pl.ds(col, count, stride=WIDE), :] = mixed[count:, :count] + mixed[:count, count:]

    block_of = lax.broadcasted_iota(jnp.int32, (WIDE, 128), 1) // TILE
    for tile in range(GROUP):
        for half in range(2):
            parts = []
            for ref in (sums_re, sums_im):
                total = jnp.zeros((WIDE, 128), jnp.float32)
                for spot in range(8):
                    at = (tile * TILE + half * 8 + spot) * WIDE
                    turned = ref[at : at + WIDE, :]
                    turn = ((spot - tile) * TILE) % 128
                    if turn:
                        turned = pltpu.roll(turned, turn, 1)
                    total = jnp.where(block_of == spot, turned, total)
                parts.append(total)
            parts = [parts[0] * peak_re - parts[1] * peak_im, parts[0] * peak_im + parts[1] * peak_re]
            out_ref[tile, :, half * 128 : (half + 1) * 128] = jnp.concatenate(parts, 0).astype(
                out_ref.dtype
            )


def field_sums(shifts, start, own, mate, table, back, coef):
    vmem = pl.BlockSpec(memory_space=pltpu.VMEM)
    smem = pl.BlockSpec(memory_space=pltpu.SMEM)
    return pl.pallas_call(
        field_kernel,
        out_shape=jax.ShapeDtypeStruct((GROUP, 2 * WIDE, TILE * TILE), jnp.bfloat16),
        in_specs=[smem, smem, vmem, vmem, pl.BlockSpec(memory_space=pl.ANY), vmem, vmem],
        out_specs=vmem,
        scratch_shapes=[
            pltpu.VMEM((2, 2, GRID // 4, 512), jnp.bfloat16),
            pltpu.SemaphoreType.DMA,
            pltpu.VMEM((4, 2 * ROWS_IN, GRID // 4), jnp.bfloat16),
            pltpu.VMEM((GRID // 128, ROWS_IN, 128), jnp.float32),
            pltpu.VMEM((GRID // 128, ROWS_IN, 128), jnp.float32),
            pltpu.VMEM((2 * WIDE, KU), jnp.bfloat16),
            pltpu.VMEM((BLOCK, KU), jnp.bfloat16),
            pltpu.VMEM((BLOCK, KU), jnp.bfloat16),
            pltpu.VMEM((TILTS * 2 * WIDE, 128), jnp.float32),
            pltpu.VMEM((TILTS * 2 * WIDE, 128), jnp.float32),
            pltpu.VMEM((GROUP * TILE * WIDE, 128), jnp.float32),
            pltpu.VMEM((GROUP * TILE * WIDE, 128), jnp.float32),
        ],
        compiler_params=pltpu.CompilerParams(vmem_limit_bytes=48 * 1024 * 1024),
    )(
        shifts,
        start,
        own,
        mate,
        table,
        back,
        coef,
    )


def probe_kernel(sums_ref, high_ref, low_ref, out_ref):
    sums = sums_ref[...].T
    probe = jnp.dot(sums, high_ref[...], preferred_element_type=jnp.float32) + jnp.dot(
        sums, low_ref[...], preferred_element_type=jnp.float32
    )
    share = out_ref.shape[1]
    real, imag = probe[:, :share], probe[:, share:]
    out_ref[...] = real * real + imag * imag


def probe_intensity(sums, high, low):
    vmem = pl.BlockSpec(memory_space=pltpu.VMEM)
    return pl.pallas_call(
        probe_kernel,
        out_shape=jax.ShapeDtypeStruct((sums.shape[1], high.shape[1] // 2), jnp.float32),
        in_specs=[vmem] * 3,
        out_specs=vmem,
        compiler_params=pltpu.CompilerParams(vmem_limit_bytes=32 * 1024 * 1024),
    )(sums, high, low)


def mixing_table(tilt_list, beam_list, beam_table, positions):
    levels = beam_table.shape[0]
    selector = (beam_list[:, None] == jnp.arange(levels, dtype=jnp.int32)[None, :]).astype(
        jnp.float32
    )
    weights = jnp.dot(selector, beam_table, precision=lax.Precision.HIGHEST)
    winding = jnp.bitwise_and(
        positions[:, 0:1] * tilt_list[None, :, 0] + positions[:, 1:2] * tilt_list[None, :, 1],
        GRID - 1,
    )
    coef_angle = two_pi * winding.astype(jnp.float32) / GRID
    cosine = jnp.cos(coef_angle)
    sine_part = jnp.sin(coef_angle)
    coef_re = weights[None, :, 0] * cosine + weights[None, :, 1] * sine_part
    coef_im = weights[None, :, 1] * cosine - weights[None, :, 0] * sine_part
    return jnp.concatenate(
        [jnp.concatenate([coef_re, -coef_im], 1), jnp.concatenate([coef_im, coef_re], 1)], 0
    ).astype(jnp.bfloat16)


def doubled(block, axis, place, strides, size):
    for stride in strides:
        other = lax.ppermute(block, axis, [(i, i ^ stride) for i in range(size)])
        upper = jnp.bitwise_and(place, stride) != 0
        block = jnp.concatenate(
            [jnp.where(upper, other, block), jnp.where(upper, block, other)], 0
        )
    return block


def groups(kind):
    flat = np.arange(64).reshape(4, 2, 2, 4)
    if kind == "depth":
        return flat.reshape(4, 16).T.tolist()
    if kind == "plane":
        return flat.reshape(4, 16).tolist()
    return flat.reshape(8, 8).tolist()


def local(potential, tilt_ids, beam_index, beam_table, positions):
    half = lax.axis_index("half")
    dev = lax.axis_index("dev")
    chip, core = half // 2, half % 2
    rows = potential.shape[0]

    first_col = chip * (2 * GROUP * WIDE) - BAND - REACH
    piece = column_piece(jnp.stack([first_col, core]).astype(jnp.int32), potential)
    piece, tilt_ids, beam_index, positions, dev = lax.optimization_barrier(
        (piece, tilt_ids, beam_index, positions, dev)
    )
    group, member = dev // GROUP, dev % GROUP
    info = jnp.concatenate([tilt_ids, beam_index[:, None]], 1)
    info = doubled(info, "half", half, (1,), HALVES)
    piece = lax.all_to_all(piece, "dev", 0, 0, tiled=True, axis_index_groups=groups("depth"))
    piece = piece.reshape(2 * rows, 2 * CHIP_COLS)
    note = jnp.concatenate([positions >> 7, jnp.bitwise_and(positions, 127)], 1)
    note = jnp.concatenate([note, jnp.zeros_like(note)], 0).astype(jnp.float32)
    windows, info = lax.optimization_barrier((windows_of(piece, note), info))
    tilt_info = doubled(info, "half", half, (2,), HALVES)
    columns = lax.all_to_all(
        windows, "dev", 0, 0, tiled=True, axis_index_groups=groups("plane")
    )
    mate = lax.ppermute(columns, "half", [(i, i ^ 1) for i in range(HALVES)])

    notes = columns[:, : positions.shape[0], 2 * ROWS_IN :].astype(jnp.int32)
    notes = lax.dynamic_slice_in_dim(notes, (group % 2) * GROUP, GROUP, 0)
    notes = notes.reshape(GROUP * positions.shape[0], NOTE)
    spots = notes[:, :2] * 128 + notes[:, 2:]
    coef = mixing_table(tilt_info[:, :2], tilt_info[:, 2], beam_table, spots)

    back = lax.dynamic_index_in_dim(jnp.asarray(back_row_table()), group, 0, keepdims=False)
    shifts = (REACH - tilt_info[:, :2]).T + jnp.stack([jnp.int32(0), WIDE * core])[:, None]
    first = WIDE * (chip * 2 * GROUP + member * 2 + core) - BAND
    zero_row = BAND + REACH - 2 * WIDE * (chip * GROUP + member)
    start = jnp.stack([first, core, zero_row]).astype(jnp.int32)
    sums = field_sums(shifts, start, columns, mate, jnp.asarray(row_table()), back, coef)

    sums = lax.all_to_all(sums, "dev", 0, 0, tiled=True, axis_index_groups=groups("tiles"))
    sums = lax.all_gather(sums, "half", axis=0, tiled=True).reshape(PARTS * 2 * WIDE, TILE * TILE)

    high, low = (
        lax.dynamic_index_in_dim(jnp.asarray(t), half, 0, keepdims=False)
        for t in back_column_table()
    )
    return probe_intensity(sums, high, low).reshape(TILE, TILE, GRID // HALVES)


def solution(mesh):
    return jax.shard_map(
        local,
        mesh=mesh,
        in_specs=(P("dev", None), P("half", None), P("half"), P(), P("dev", None)),
        out_specs=P("dev", None, "half"),
        check_vma=False,
    )
```

```python
import functools
import math

import jax
import jax.numpy as jnp
import ml_dtypes
import numpy as np
from jax import lax
from jax.experimental import pallas as pl
from jax.experimental.pallas import tpu as pltpu
from jax.sharding import PartitionSpec as P

two_pi = 2.0 * math.pi
propagation_rate = 0.6

GRID = 1024
TILTS = 256
REACH = 128
BAND = 341
GROUP = 8
HALVES = 4
TILE = 16
WIDE = 24
PARTS = GROUP * HALVES
PART_ROWS = GROUP * 2 * WIDE
ROWS_IN = 2 * WIDE + 2 * REACH
CHIP_COLS = GROUP * 2 * WIDE + 2 * REACH
NOTE = 4
LANES = 2 * ROWS_IN + NOTE
KU = 768
BATCH = 16
BLOCK = 2 * BATCH * WIDE
STEP = 2 * WIDE + 1


def spread_of(row, xnp=np):
    turn = row * 0.6180339887498949
    return xnp.exp2(turn - xnp.floor(turn))


def angles(product):
    return np.mod(product, GRID).astype(np.float64) * (2.0 * np.pi / GRID)


def two_parts(table):
    high = table.astype(np.float32).astype(ml_dtypes.bfloat16)
    low = (table - high.astype(np.float64)).astype(np.float32).astype(ml_dtypes.bfloat16)
    return high, low


@functools.lru_cache(maxsize=None)
def column_table():
    angle = angles(np.arange(GRID)[:, None] * np.arange(128)[None, :])
    return np.stack(two_parts(np.concatenate([np.cos(angle), np.sin(angle)], 1)))


@functools.lru_cache(maxsize=None)
def row_table():
    core, pair, source, depth, inner = np.meshgrid(
        np.arange(2), np.arange(2), np.arange(16), np.arange(4), np.arange(4), indexing="ij"
    )
    inner = 4 * inner + 2 * pair + core
    rows = ((depth * 16 + source) * TILE + inner).reshape(4, GRID // 4)
    angle = angles(rows[:, :, None] * (np.arange(GRID // 4) - BAND - REACH)[None, None, :])
    table = np.stack([np.cos(angle), np.sin(angle)], 2)
    table = table / spread_of(rows % TILE)[:, :, None, None]
    table = table.reshape(2, 2, GRID // 4, 2, 2, 128).transpose(0, 1, 2, 4, 3, 5)
    return table.reshape(2, 2, GRID // 4, 512).astype(np.float32).astype(ml_dtypes.bfloat16)


@functools.lru_cache(maxsize=None)
def back_row_table():
    index = np.arange(KU) - BAND
    result = []
    for group in range(8):
        rows = np.arange(GROUP * TILE) + group * GROUP * TILE
        angle = angles(index[:, None] * rows[None, :])
        angle = angle - (propagation_rate / GRID) * (index * index).astype(np.float64)[:, None]
        cosine, sine = np.cos(angle), np.sin(angle)
        result.append(np.concatenate([cosine, sine], 1))
    return np.stack(result).astype(np.float32).astype(ml_dtypes.bfloat16)


@functools.lru_cache(maxsize=None)
def back_column_table():
    chip, core, member = np.meshgrid(np.arange(2), np.arange(2), np.arange(GROUP), indexing="ij")
    part = (chip * 2 * GROUP + member * 2 + core).reshape(-1)
    index = (part[:, None] * WIDE + np.arange(WIDE)[None, :]).reshape(-1) - BAND
    cols = np.arange(GRID // HALVES)
    angle = angles(index[:, None] * cols[None, :])
    angle = angle - (propagation_rate / GRID) * (index * index).astype(np.float64)[:, None]
    scale = 1.0 / (GRID * GRID)
    cosine = (np.cos(angle) * scale).reshape(PARTS, WIDE, -1)
    sine = (np.sin(angle) * scale).reshape(PARTS, WIDE, -1)
    table = np.concatenate(
        [np.concatenate([cosine, sine], 2), np.concatenate([-sine, cosine], 2)], 1
    )
    return two_parts(table.reshape(HALVES, PART_ROWS, 2 * GRID // HALVES))


def chosen(rows, cols, source):
    row = lax.broadcasted_iota(jnp.int32, (rows, cols), 0)
    col = lax.broadcasted_iota(jnp.int32, (rows, cols), 1)
    return jnp.where(col == source(row), 1.0, 0.0).astype(jnp.bfloat16)


def column_kernel(field_ref, table_ref, out_ref, field_in, table, arrived):
    copies = [
        pltpu.make_async_copy(field_ref, field_in, arrived.at[0]),
        pltpu.make_async_copy(table_ref, table, arrived.at[1]),
    ]
    for copy in copies:
        copy.start()
    half = lax.axis_index("half")
    chip, core = half // 2, half % 2
    first = chip * (2 * GROUP * WIDE) - BAND - REACH
    rows = field_in.shape[0] // 2
    pick = chosen(rows, 2 * rows, lambda row: 4 * (row % 4) + 2 * (row // 4) + core)
    row = lax.broadcasted_iota(jnp.int32, (rows, 128), 0)
    spread = spread_of(4 * (row % 4) + 2 * (row // 4) + core, jnp)[:, :1]
    copies[0].wait()
    field = jnp.dot(pick, field_in[...], preferred_element_type=jnp.float32)
    column = lax.broadcasted_iota(jnp.int32, (rows, GRID), 1)
    turn = jnp.bitwise_and(first * column, GRID - 1)
    phase = field - (two_pi / GRID) * turn.astype(jnp.float32)
    cosine, sine = jnp.cos(phase) * spread, jnp.sin(phase) * spread
    waves = [cosine, sine]
    column = column[:, :128]
    for chunk in range(1, CHIP_COLS // 128):
        eighth = jnp.bitwise_and(chunk * column, 7).astype(jnp.float32) * (two_pi / 8)
        turn_re, turn_im = (
            jnp.concatenate([x] * (GRID // 128), 1) for x in (jnp.cos(eighth), jnp.sin(eighth))
        )
        waves += [cosine * turn_re + sine * turn_im, sine * turn_re - cosine * turn_im]
    wave = jnp.concatenate(waves, 0)
    high = wave.astype(jnp.bfloat16)
    low = (wave - high.astype(jnp.float32)).astype(jnp.bfloat16)
    count = wave.shape[0]
    copies[1].wait()
    both = jnp.dot(jnp.concatenate([high, low], 0), table[0], preferred_element_type=jnp.float32)
    mixed = both[:count] + both[count:]
    mixed = mixed + jnp.dot(high, table[1], preferred_element_type=jnp.float32)
    cols_re, cols_im = [], []
    for chunk in range(CHIP_COLS // 128):
        cosine = mixed[2 * rows * chunk : 2 * rows * chunk + rows]
        sine = mixed[2 * rows * chunk + rows : 2 * rows * (chunk + 1)]
        cols_re.append(cosine[:, :128] + sine[:, 128:])
        cols_im.append(sine[:, :128] - cosine[:, 128:])
    piece = jnp.concatenate(cols_re + cols_im, 1).astype(jnp.bfloat16)
    for copy in range(out_ref.shape[0]):
        out_ref[copy] = piece


def column_piece(potential):
    vmem = pl.BlockSpec(memory_space=pltpu.VMEM)
    table = column_table()
    rows = potential.shape[0]
    anywhere = pl.BlockSpec(memory_space=pltpu.HBM)
    return pl.pallas_call(
        column_kernel,
        out_shape=jax.ShapeDtypeStruct((4, rows // 2, 2 * CHIP_COLS), jnp.bfloat16),
        in_specs=[anywhere, anywhere],
        out_specs=vmem,
        scratch_shapes=[
            pltpu.VMEM(potential.shape, jnp.bfloat16),
            pltpu.VMEM(table.shape, jnp.bfloat16),
            pltpu.SemaphoreType.DMA((2,)),
        ],
        compiler_params=pltpu.CompilerParams(vmem_limit_bytes=56 * 1024 * 1024),
    )(potential, jnp.asarray(table))


def window_kernel(piece_ref, spot_ref, out_ref):
    rows = piece_ref.shape[0]
    pick = chosen(rows, rows, lambda row: 8 * ((row // 4) % 4) + 4 * (row // 16) + row % 4)
    piece = jnp.dot(pick, piece_ref[...], preferred_element_type=jnp.float32)
    spots = spot_ref[...]
    note = jnp.concatenate([spots >> 7, jnp.bitwise_and(spots, 127)], 1).astype(jnp.float32)
    note = jnp.concatenate([note, jnp.zeros_like(note)], 0)
    for member in range(GROUP):
        at = 2 * WIDE * member
        window = jnp.concatenate(
            [piece[:, part * CHIP_COLS + at : part * CHIP_COLS + at + ROWS_IN] for part in range(2)]
            + [note],
            1,
        ).astype(jnp.bfloat16)
        for copy in range(2):
            out_ref[member + copy * GROUP] = window


def windows_of(piece, spots):
    vmem = pl.BlockSpec(memory_space=pltpu.VMEM)
    return pl.pallas_call(
        window_kernel,
        out_shape=jax.ShapeDtypeStruct((2 * GROUP, piece.shape[0], LANES), jnp.bfloat16),
        in_specs=[vmem, vmem],
        out_specs=vmem,
        compiler_params=pltpu.CompilerParams(vmem_limit_bytes=16 * 1024 * 1024),
    )(piece, spots)


def field_kernel(
    shift_ref,
    start_ref,
    own_ref,
    mate_ref,
    own_table,
    mate_table,
    back_ref,
    coef_ref,
    out_ref,
    turned_ref,
    spec_re,
    spec_im,
    mask,
    rows_a,
    rows_b,
    field_re,
    field_im,
    sums_re,
    sums_im,
):
    first_core = start_ref[1] == 0
    for pair in range(2):
        for place, ref in enumerate((own_ref, mate_ref)):
            block = ref[:, 16 * pair : 16 * pair + 16, :]
            block = block.reshape(GRID // 4, LANES)[:, : 2 * ROWS_IN]
            turned_ref[2 * place + pair] = block.T
    for part in range(2):
        lanes = slice(256 * part, 256 * (part + 1))
        each = []
        for place, ref in enumerate((own_table, mate_table)):
            for pair in range(2):
                both = jnp.dot(
                    turned_ref[2 * place + pair],
                    ref[pair, :, lanes],
                    preferred_element_type=jnp.float32,
                )
                each.append(
                    (
                        both[:ROWS_IN, :128] + both[ROWS_IN:, 128:],
                        both[ROWS_IN:, :128] - both[:ROWS_IN, 128:],
                    )
                )
        each = [
            tuple(jnp.where(first_core, x, y) for x, y in zip(each[one], each[two]))
            for one, two in ((0, 2), (2, 0), (1, 3), (3, 1))
        ]
        (re0, im0), (re1, im1), (re2, im2), (re3, im3) = each
        even, even_less = (re0 + re2, im0 + im2), (re0 - re2, im0 - im2)
        odd, odd_less = (re1 + re3, im1 + im3), (im1 - im3, re3 - re1)
        for quarter, left, right, sign in (
            (0, even, odd, 1),
            (1, even_less, odd_less, 1),
            (2, even, odd, -1),
            (3, even_less, odd_less, -1),
        ):
            for ref, x, y in ((spec_re, left[0], right[0]), (spec_im, left[1], right[1])):
                ref[2 * quarter + part] = x + y if sign > 0 else x - y

    peak_row = start_ref[2]
    peak_at = jnp.clip(peak_row, 0, ROWS_IN - 1)
    peak_lane = BAND + REACH
    peak_re, peak_im = (
        ref[peak_lane // 128, pl.ds(peak_at, 1), :][:, peak_lane % 128 : peak_lane % 128 + 1]
        for ref in (spec_re, spec_im)
    )
    power = peak_re * peak_re + peak_im * peak_im
    held = jnp.logical_and(power > 1e-6, peak_row == peak_at)
    peak_re = jnp.where(held, peak_re, 1.0)
    peak_im = jnp.where(held, peak_im, 0.0)
    inverse = 1.0 / jnp.where(held, power, 1.0)
    scale_re, scale_im = peak_re * inverse, -peak_im * inverse
    for chunk in range(GRID // 128):
        value_re, value_im = spec_re[chunk], spec_im[chunk]
        spec_re[chunk] = value_re * scale_re - value_im * scale_im
        spec_im[chunk] = value_re * scale_im + value_im * scale_re

    first = start_ref[0]
    row_index = lax.broadcasted_iota(jnp.int32, (WIDE, KU), 0) + first
    lane_index = lax.broadcasted_iota(jnp.int32, (WIDE, KU), 1) - BAND
    inside = 9 * (row_index * row_index + lane_index * lane_index) < GRID * GRID
    inside = jnp.where(inside, 1.0, 0.0)
    mask[...] = jnp.concatenate([inside, inside], 0).astype(jnp.bfloat16)
    chunks = KU // 128

    def shifted(tilt, rows, at):
        row_at = shift_ref[1, tilt]
        lane_at = shift_ref[0, tilt]
        base = jnp.where(lane_at >= 128, 1, 0)
        rest = lane_at - 128 * base
        lanes = lax.broadcasted_iota(jnp.int32, (2 * WIDE, 128), 1)
        keep = lanes < 128 - rest
        turn = jnp.bitwise_and(128 - rest, 127)
        before = None
        for chunk in range(chunks + 1):
            window = jnp.concatenate(
                [ref[base + chunk, pl.ds(row_at, WIDE), :] for ref in (spec_re, spec_im)], 0
            )
            rolled = pltpu.roll(window.astype(jnp.bfloat16), turn, 1)
            if chunk:
                lanes_at = (chunk - 1) * 128
                rows[at : at + 2 * WIDE, lanes_at : lanes_at + 128] = (
                    jnp.where(keep, before, rolled) * mask[:, lanes_at : lanes_at + 128]
                )
            before = rolled

    def fill(step, rows):
        for spot in range(BATCH):
            shifted(step * BATCH + spot, rows, spot * 2 * WIDE)

    def multiply(step, rows):
        result = jnp.dot(rows[...], back_ref[...], preferred_element_type=jnp.float32)
        for spot in range(BATCH):
            at = step * BATCH * STEP + spot * STEP
            piece = result[spot * 2 * WIDE : (spot + 1) * 2 * WIDE]
            field_re[pl.ds(at, 2 * WIDE), :] = piece[:, :128]
            field_im[pl.ds(at, 2 * WIDE), :] = piece[:, 128:]

    steps = TILTS // BATCH
    fill(0, rows_a)

    def block(turn, carry):
        fill(2 * turn + 1, rows_b)
        multiply(2 * turn, rows_a)
        fill(jnp.minimum(2 * turn + 2, steps - 1), rows_a)
        multiply(2 * turn + 1, rows_b)
        return carry

    lax.fori_loop(0, steps // 2, block, 0)

    count = GROUP * TILE
    for col in range(WIDE):
        values = jnp.concatenate(
            [
                jnp.concatenate(
                    [ref[pl.ds(col + WIDE * part, TILTS, stride=STEP), :] for part in range(2)], 0
                ).astype(jnp.bfloat16)
                for ref in (field_re, field_im)
            ],
            1,
        )
        mixed = jnp.dot(coef_ref[...], values, preferred_element_type=jnp.float32)
        sums_re[pl.ds(col, count, stride=WIDE), :] = mixed[:count, :count] - mixed[count:, count:]
        sums_im[pl.ds(col, count, stride=WIDE), :] = mixed[count:, :count] + mixed[:count, count:]

    block_of = lax.broadcasted_iota(jnp.int32, (WIDE, 128), 1) // TILE
    for tile in range(GROUP):
        for half in range(2):
            parts = []
            for ref in (sums_re, sums_im):
                total = jnp.zeros((WIDE, 128), jnp.float32)
                for spot in range(8):
                    at = (tile * TILE + half * 8 + spot) * WIDE
                    turned = ref[at : at + WIDE, :]
                    turn = ((spot - tile) * TILE) % 128
                    if turn:
                        turned = pltpu.roll(turned, turn, 1)
                    total = jnp.where(block_of == spot, turned, total)
                parts.append(total)
            parts = [parts[0] * peak_re - parts[1] * peak_im, parts[0] * peak_im + parts[1] * peak_re]
            parts = jnp.concatenate(parts, 0).astype(out_ref.dtype)
            for copy in range(2):
                out_ref[tile + copy * GROUP, :, half * 128 : (half + 1) * 128] = parts


def field_sums(shifts, start, own, mate, own_table, mate_table, back, coef):
    vmem = pl.BlockSpec(memory_space=pltpu.VMEM)
    smem = pl.BlockSpec(memory_space=pltpu.SMEM)
    return pl.pallas_call(
        field_kernel,
        out_shape=jax.ShapeDtypeStruct((2 * GROUP, 2 * WIDE, TILE * TILE), jnp.bfloat16),
        in_specs=[smem, smem] + [vmem] * 6,
        out_specs=vmem,
        scratch_shapes=[
            pltpu.VMEM((4, 2 * ROWS_IN, GRID // 4), jnp.bfloat16),
            pltpu.VMEM((GRID // 128, ROWS_IN, 128), jnp.float32),
            pltpu.VMEM((GRID // 128, ROWS_IN, 128), jnp.float32),
            pltpu.VMEM((2 * WIDE, KU), jnp.bfloat16),
            pltpu.VMEM((BLOCK, KU), jnp.bfloat16),
            pltpu.VMEM((BLOCK, KU), jnp.bfloat16),
            pltpu.VMEM((TILTS * STEP, 128), jnp.float32),
            pltpu.VMEM((TILTS * STEP, 128), jnp.float32),
            pltpu.VMEM((GROUP * TILE * WIDE, 128), jnp.float32),
            pltpu.VMEM((GROUP * TILE * WIDE, 128), jnp.float32),
        ],
        compiler_params=pltpu.CompilerParams(vmem_limit_bytes=30 * 1024 * 1024),
    )(
        shifts,
        start,
        own,
        mate,
        own_table,
        mate_table,
        back,
        coef,
    )


def probe_kernel(half_ref, own_ref, mate_ref, high_ref, low_ref, out_ref):
    half = half_ref[0]
    index = lax.broadcasted_iota(jnp.int32, (1, WIDE, TILE * TILE), 1) + (3 * BAND)
    turns = jnp.bitwise_and(index * half, 3)
    cosine = jnp.where(turns == 0, 1.0, jnp.where(turns == 2, -1.0, 0.0))
    sine = jnp.where(turns == 1, 1.0, jnp.where(turns == 3, -1.0, 0.0))
    probe = 0.0
    for ref, core in ((own_ref, half % 2), (mate_ref, 1 - half % 2)):
        for chip in range(2):
            sums = ref[chip].astype(jnp.float32)
            real, imag = sums[:, :WIDE], sums[:, WIDE:]
            sums = jnp.concatenate([real * cosine - imag * sine, real * sine + imag * cosine], 1)
            sums = sums.reshape(PART_ROWS, TILE * TILE).T.astype(jnp.bfloat16)
            part = 2 * chip + core
            probe = probe + jnp.dot(sums, high_ref[part], preferred_element_type=jnp.float32)
            probe = probe + jnp.dot(sums, low_ref[part], preferred_element_type=jnp.float32)
    share = out_ref.shape[1]
    real, imag = probe[:, :share], probe[:, share:]
    out_ref[...] = real * real + imag * imag


def probe_all(half, own, mate, high, low):
    vmem = pl.BlockSpec(memory_space=pltpu.VMEM)
    smem = pl.BlockSpec(memory_space=pltpu.SMEM)
    return pl.pallas_call(
        probe_kernel,
        out_shape=jax.ShapeDtypeStruct((TILE * TILE, GRID // HALVES), jnp.float32),
        in_specs=[smem] + [vmem] * 4,
        out_specs=vmem,
        compiler_params=pltpu.CompilerParams(vmem_limit_bytes=24 * 1024 * 1024),
    )(half, own, mate, high, low)


def mixing_table(tilt_list, beam_list, beam_table, positions):
    levels = beam_table.shape[0]
    selector = (beam_list[:, None] == jnp.arange(levels, dtype=jnp.int32)[None, :]).astype(
        jnp.float32
    )
    weights = jnp.dot(selector, beam_table, precision=lax.Precision.HIGHEST)
    winding = jnp.bitwise_and(
        positions[:, 0:1] * tilt_list[None, :, 0] + positions[:, 1:2] * tilt_list[None, :, 1],
        GRID - 1,
    )
    coef_angle = two_pi * winding.astype(jnp.float32) / GRID
    cosine = jnp.cos(coef_angle)
    sine_part = jnp.sin(coef_angle)
    coef_re = weights[None, :, 0] * cosine + weights[None, :, 1] * sine_part
    coef_im = weights[None, :, 1] * cosine - weights[None, :, 0] * sine_part
    return jnp.concatenate(
        [jnp.concatenate([coef_re, -coef_im], 1), jnp.concatenate([coef_im, coef_re], 1)], 0
    ).astype(jnp.bfloat16)


def doubled(block, axis, place, strides, size):
    for stride in strides:
        other = lax.ppermute(block, axis, [(i, i ^ stride) for i in range(size)])
        upper = jnp.bitwise_and(place, stride) != 0
        block = jnp.concatenate(
            [jnp.where(upper, other, block), jnp.where(upper, block, other)], 0
        )
    return block


def groups(kind):
    flat = np.arange(64).reshape(4, 2, 2, 4)
    if kind == "depth":
        return flat.reshape(4, 16).T.tolist()
    if kind == "plane":
        return flat.reshape(4, 16).tolist()
    return flat.reshape(8, 8).tolist()


def joint_groups():
    flat = np.arange(256).reshape(2, 2, 8, 8)
    return flat.transpose(2, 1, 0, 3).reshape(16, 16).tolist()


def local(potential, tilt_ids, beam_index, beam_table, positions):
    half = lax.axis_index("half")
    dev = lax.axis_index("dev")
    chip, core = half // 2, half % 2
    rows = potential.shape[0]

    piece = column_piece(potential)
    piece = lax.all_to_all(piece, "dev", 0, 0, tiled=True, axis_index_groups=groups("depth"))
    windows = windows_of(piece.reshape(2 * rows, 2 * CHIP_COLS), positions)
    windows, tilt_ids, beam_index, dev, core_late = lax.optimization_barrier(
        (windows, tilt_ids, beam_index, dev, core)
    )
    group, member = dev // GROUP, dev % GROUP
    info = jnp.concatenate([tilt_ids, beam_index[:, None]], 1)
    tilt_info = doubled(info, "half", half, (1, 2), HALVES)
    columns = lax.all_to_all(
        windows, "dev", 0, 0, tiled=True, axis_index_groups=groups("plane")
    )
    mate = lax.ppermute(columns, "half", [(i, i ^ 1) for i in range(HALVES)])

    notes = columns[:, : positions.shape[0], 2 * ROWS_IN :].astype(jnp.int32)
    notes = lax.dynamic_slice_in_dim(notes, (group % 2) * GROUP, GROUP, 0)
    notes = notes.reshape(GROUP * positions.shape[0], NOTE)
    spots = notes[:, :2] * 128 + notes[:, 2:]
    coef = mixing_table(tilt_info[:, :2], tilt_info[:, 2], beam_table, spots)

    row_tables = [
        lax.dynamic_index_in_dim(jnp.asarray(row_table()), place, 0, keepdims=False)
        for place in (core_late, 1 - core_late)
    ]
    back = lax.dynamic_index_in_dim(jnp.asarray(back_row_table()), group, 0, keepdims=False)
    shifts = (REACH - tilt_info[:, :2]).T + jnp.stack([jnp.int32(0), WIDE * core])[:, None]
    first = WIDE * (chip * 2 * GROUP + member * 2 + core) - BAND
    zero_row = BAND + REACH - 2 * WIDE * (chip * GROUP + member)
    start = jnp.stack([first, core, zero_row]).astype(jnp.int32)
    sums = field_sums(shifts, start, columns, mate, *row_tables, back, coef)

    sums = lax.all_to_all(
        sums,
        ("half", "dev"), 0, 0, tiled=True, axis_index_groups=joint_groups(),
    )
    mates = lax.ppermute(sums, "half", [(i, i ^ 1) for i in range(HALVES)])
    sums, mates = (x.reshape(2, GROUP, 2 * WIDE, TILE * TILE) for x in (sums, mates))

    high, low = (jnp.asarray(t) for t in back_column_table())
    place = half.reshape(1)
    probe = probe_all(place, sums, mates, high, low)
    return probe.reshape(TILE, TILE, GRID // HALVES)


def solution(mesh):
    return jax.shard_map(
        local,
        mesh=mesh,
        in_specs=(P("dev", None), P("half", None), P("half"), P(), P("dev", None)),
        out_specs=P("dev", None, "half"),
        check_vma=False,
    )
```

```python
import functools
import math

import jax
import jax.numpy as jnp
import ml_dtypes
import numpy as np
from jax import lax
from jax.experimental import pallas as pl
from jax.experimental.pallas import tpu as pltpu
from jax.sharding import PartitionSpec as P

two_pi = 2.0 * math.pi
propagation_rate = 0.6

GRID = 1024
TILTS = 256
REACH = 128
BAND = 341
GROUP = 8
HALVES = 4
TILE = 16
WIDE = 24
PARTS = GROUP * HALVES
PART_ROWS = GROUP * 2 * WIDE
ROWS_IN = 2 * WIDE + 2 * REACH
CHIP_COLS = GROUP * 2 * WIDE + 2 * REACH
NOTE = 4
LANES = 2 * ROWS_IN + NOTE
KU = 768
BATCH = 16
BLOCK = 2 * BATCH * WIDE
STEP = 2 * WIDE + 1


def spread_of(row, xnp=np):
    turn = row * 0.6180339887498949
    return xnp.exp2(turn - xnp.floor(turn))


def angles(product):
    return np.mod(product, GRID).astype(np.float64) * (2.0 * np.pi / GRID)


def two_parts(table):
    high = table.astype(np.float32).astype(ml_dtypes.bfloat16)
    low = (table - high.astype(np.float64)).astype(np.float32).astype(ml_dtypes.bfloat16)
    return high, low


@functools.lru_cache(maxsize=None)
def column_table():
    angle = angles(np.arange(GRID)[:, None] * np.arange(128)[None, :])
    return np.stack(two_parts(np.concatenate([np.cos(angle), np.sin(angle)], 1)))


@functools.lru_cache(maxsize=None)
def row_table():
    core, pair, source, depth, inner = np.meshgrid(
        np.arange(2), np.arange(2), np.arange(16), np.arange(4), np.arange(4), indexing="ij"
    )
    inner = 4 * inner + 2 * pair + core
    rows = ((depth * 16 + source) * TILE + inner).reshape(4, GRID // 4)
    angle = angles(rows[:, :, None] * (np.arange(GRID // 4) - BAND - REACH)[None, None, :])
    table = np.stack([np.cos(angle), np.sin(angle)], 2)
    table = table / spread_of(rows % TILE)[:, :, None, None]
    table = table.reshape(2, 2, GRID // 4, 2, 2, 128).transpose(0, 1, 2, 4, 3, 5)
    return table.reshape(2, 2, GRID // 4, 512).astype(np.float32).astype(ml_dtypes.bfloat16)


@functools.lru_cache(maxsize=None)
def back_row_table():
    index = np.arange(KU) - BAND
    result = []
    for group in range(8):
        rows = np.arange(GROUP * TILE) + group * GROUP * TILE
        angle = angles(index[:, None] * rows[None, :])
        angle = angle - (propagation_rate / GRID) * (index * index).astype(np.float64)[:, None]
        cosine, sine = np.cos(angle), np.sin(angle)
        result.append(np.concatenate([cosine, sine], 1))
    return np.stack(result).astype(np.float32).astype(ml_dtypes.bfloat16)


@functools.lru_cache(maxsize=None)
def back_column_table():
    core, chip, member = np.meshgrid(np.arange(2), np.arange(2), np.arange(GROUP), indexing="ij")
    part = (chip * 2 * GROUP + member * 2 + core).reshape(-1)
    index = (part[:, None] * WIDE + np.arange(WIDE)[None, :]).reshape(-1) - BAND
    cols = np.arange(GRID // HALVES)
    angle = angles(index[:, None] * cols[None, :])
    angle = angle - (propagation_rate / GRID) * (index * index).astype(np.float64)[:, None]
    scale = 1.0 / (GRID * GRID)
    return two_parts(np.concatenate([np.cos(angle), np.sin(angle)], 1) * scale)


def chosen(rows, cols, source):
    row = lax.broadcasted_iota(jnp.int32, (rows, cols), 0)
    col = lax.broadcasted_iota(jnp.int32, (rows, cols), 1)
    return jnp.where(col == source(row), 1.0, 0.0).astype(jnp.bfloat16)


def column_kernel(field_ref, table_ref, out_ref, field_in, table, arrived):
    copies = [
        pltpu.make_async_copy(field_ref, field_in, arrived.at[0]),
        pltpu.make_async_copy(table_ref, table, arrived.at[1]),
    ]
    for copy in copies:
        copy.start()
    half = lax.axis_index("half")
    chip, core = half // 2, half % 2
    first = chip * (2 * GROUP * WIDE) - BAND - REACH
    rows = field_in.shape[0] // 2
    pick = chosen(rows, 2 * rows, lambda row: 4 * (row % 4) + 2 * (row // 4) + core)
    row = lax.broadcasted_iota(jnp.int32, (rows, 128), 0)
    spread = spread_of(4 * (row % 4) + 2 * (row // 4) + core, jnp)[:, :1]
    copies[0].wait()
    field = jnp.dot(pick, field_in[...], preferred_element_type=jnp.float32)
    column = lax.broadcasted_iota(jnp.int32, (rows, GRID), 1)
    turn = jnp.bitwise_and(first * column, GRID - 1)
    phase = field - (two_pi / GRID) * turn.astype(jnp.float32)
    cosine, sine = jnp.cos(phase) * spread, jnp.sin(phase) * spread
    waves = [cosine, sine]
    column = column[:, :128]
    for chunk in range(1, CHIP_COLS // 128):
        eighth = jnp.bitwise_and(chunk * column, 7).astype(jnp.float32) * (two_pi / 8)
        turn_re, turn_im = (
            jnp.concatenate([x] * (GRID // 128), 1) for x in (jnp.cos(eighth), jnp.sin(eighth))
        )
        waves += [cosine * turn_re + sine * turn_im, sine * turn_re - cosine * turn_im]
    wave = jnp.concatenate(waves, 0)
    high = wave.astype(jnp.bfloat16)
    low = (wave - high.astype(jnp.float32)).astype(jnp.bfloat16)
    count = wave.shape[0]
    copies[1].wait()
    both = jnp.dot(jnp.concatenate([high, low], 0), table[0], preferred_element_type=jnp.float32)
    mixed = both[:count] + both[count:]
    mixed = mixed + jnp.dot(high, table[1], preferred_element_type=jnp.float32)
    cols_re, cols_im = [], []
    for chunk in range(CHIP_COLS // 128):
        cosine = mixed[2 * rows * chunk : 2 * rows * chunk + rows]
        sine = mixed[2 * rows * chunk + rows : 2 * rows * (chunk + 1)]
        cols_re.append(cosine[:, :128] + sine[:, 128:])
        cols_im.append(sine[:, :128] - cosine[:, 128:])
    piece = jnp.concatenate(cols_re + cols_im, 1).astype(jnp.bfloat16)
    for copy in range(out_ref.shape[0]):
        out_ref[copy] = piece


def column_piece(potential):
    vmem = pl.BlockSpec(memory_space=pltpu.VMEM)
    table = column_table()
    rows = potential.shape[0]
    anywhere = pl.BlockSpec(memory_space=pltpu.HBM)
    return pl.pallas_call(
        column_kernel,
        out_shape=jax.ShapeDtypeStruct((4, rows // 2, 2 * CHIP_COLS), jnp.bfloat16),
        in_specs=[anywhere, anywhere],
        out_specs=vmem,
        scratch_shapes=[
            pltpu.VMEM(potential.shape, jnp.bfloat16),
            pltpu.VMEM(table.shape, jnp.bfloat16),
            pltpu.SemaphoreType.DMA((2,)),
        ],
        compiler_params=pltpu.CompilerParams(vmem_limit_bytes=56 * 1024 * 1024),
    )(potential, jnp.asarray(table))


def window_kernel(piece_ref, spot_ref, out_ref):
    rows = piece_ref.shape[0]
    pick = chosen(rows, rows, lambda row: 8 * ((row // 4) % 4) + 4 * (row // 16) + row % 4)
    piece = jnp.dot(pick, piece_ref[...], preferred_element_type=jnp.float32)
    spots = spot_ref[...]
    note = jnp.concatenate([spots >> 7, jnp.bitwise_and(spots, 127)], 1).astype(jnp.float32)
    note = jnp.concatenate([note, jnp.zeros_like(note)], 0)
    for member in range(GROUP):
        at = 2 * WIDE * member
        window = jnp.concatenate(
            [piece[:, part * CHIP_COLS + at : part * CHIP_COLS + at + ROWS_IN] for part in range(2)]
            + [note],
            1,
        ).astype(jnp.bfloat16)
        for copy in range(2):
            out_ref[member + copy * GROUP] = window


def windows_of(piece, spots):
    vmem = pl.BlockSpec(memory_space=pltpu.VMEM)
    return pl.pallas_call(
        window_kernel,
        out_shape=jax.ShapeDtypeStruct((2 * GROUP, piece.shape[0], LANES), jnp.bfloat16),
        in_specs=[vmem, vmem],
        out_specs=vmem,
        compiler_params=pltpu.CompilerParams(vmem_limit_bytes=16 * 1024 * 1024),
    )(piece, spots)


def field_kernel(
    shift_ref,
    start_ref,
    own_ref,
    mate_ref,
    own_table,
    mate_table,
    back_ref,
    coef_ref,
    out_ref,
    turned_ref,
    spec_re,
    spec_im,
    mask,
    rows_a,
    rows_b,
    field_re,
    field_im,
    sums_re,
    sums_im,
):
    first_core = start_ref[1] == 0
    for pair in range(2):
        for place, ref in enumerate((own_ref, mate_ref)):
            block = ref[:, 16 * pair : 16 * pair + 16, :]
            block = block.reshape(GRID // 4, LANES)[:, : 2 * ROWS_IN]
            turned_ref[2 * place + pair] = block.T
    for part in range(2):
        lanes = slice(256 * part, 256 * (part + 1))
        each = []
        for place, ref in enumerate((own_table, mate_table)):
            for pair in range(2):
                both = jnp.dot(
                    turned_ref[2 * place + pair],
                    ref[pair, :, lanes],
                    preferred_element_type=jnp.float32,
                )
                each.append(
                    (
                        both[:ROWS_IN, :128] + both[ROWS_IN:, 128:],
                        both[ROWS_IN:, :128] - both[:ROWS_IN, 128:],
                    )
                )
        each = [
            tuple(jnp.where(first_core, x, y) for x, y in zip(each[one], each[two]))
            for one, two in ((0, 2), (2, 0), (1, 3), (3, 1))
        ]
        (re0, im0), (re1, im1), (re2, im2), (re3, im3) = each
        even, even_less = (re0 + re2, im0 + im2), (re0 - re2, im0 - im2)
        odd, odd_less = (re1 + re3, im1 + im3), (im1 - im3, re3 - re1)
        for quarter, left, right, sign in (
            (0, even, odd, 1),
            (1, even_less, odd_less, 1),
            (2, even, odd, -1),
            (3, even_less, odd_less, -1),
        ):
            for ref, x, y in ((spec_re, left[0], right[0]), (spec_im, left[1], right[1])):
                ref[2 * quarter + part] = x + y if sign > 0 else x - y

    peak_row = start_ref[2]
    peak_at = jnp.clip(peak_row, 0, ROWS_IN - 1)
    peak_lane = BAND + REACH
    peak_re, peak_im = (
        ref[peak_lane // 128, pl.ds(peak_at, 1), :][:, peak_lane % 128 : peak_lane % 128 + 1]
        for ref in (spec_re, spec_im)
    )
    power = peak_re * peak_re + peak_im * peak_im
    held = jnp.logical_and(power > 1e-6, peak_row == peak_at)
    peak_re = jnp.where(held, peak_re, 1.0)
    peak_im = jnp.where(held, peak_im, 0.0)
    inverse = 1.0 / jnp.where(held, power, 1.0)
    scale_re, scale_im = peak_re * inverse, -peak_im * inverse
    for chunk in range(GRID // 128):
        value_re, value_im = spec_re[chunk], spec_im[chunk]
        spec_re[chunk] = value_re * scale_re - value_im * scale_im
        spec_im[chunk] = value_re * scale_im + value_im * scale_re

    first = start_ref[0]
    row_index = lax.broadcasted_iota(jnp.int32, (WIDE, KU), 0) + first
    lane_index = lax.broadcasted_iota(jnp.int32, (WIDE, KU), 1) - BAND
    inside = 9 * (row_index * row_index + lane_index * lane_index) < GRID * GRID
    inside = jnp.where(inside, 1.0, 0.0)
    mask[...] = jnp.concatenate([inside, inside], 0).astype(jnp.bfloat16)
    chunks = KU // 128

    def shifted(tilt, rows, at):
        row_at = shift_ref[1, tilt]
        lane_at = shift_ref[0, tilt]
        base = jnp.where(lane_at >= 128, 1, 0)
        rest = lane_at - 128 * base
        lanes = lax.broadcasted_iota(jnp.int32, (2 * WIDE, 128), 1)
        keep = lanes < 128 - rest
        turn = jnp.bitwise_and(128 - rest, 127)
        before = None
        for chunk in range(chunks + 1):
            window = jnp.concatenate(
                [ref[base + chunk, pl.ds(row_at, WIDE), :] for ref in (spec_re, spec_im)], 0
            )
            rolled = pltpu.roll(window.astype(jnp.bfloat16), turn, 1)
            if chunk:
                lanes_at = (chunk - 1) * 128
                rows[at : at + 2 * WIDE, lanes_at : lanes_at + 128] = (
                    jnp.where(keep, before, rolled) * mask[:, lanes_at : lanes_at + 128]
                )
            before = rolled

    def fill(step, rows):
        for spot in range(BATCH):
            shifted(step * BATCH + spot, rows, spot * 2 * WIDE)

    def multiply(step, rows):
        result = jnp.dot(rows[...], back_ref[...], preferred_element_type=jnp.float32)
        for spot in range(BATCH):
            at = step * BATCH * STEP + spot * STEP
            piece = result[spot * 2 * WIDE : (spot + 1) * 2 * WIDE]
            field_re[pl.ds(at, 2 * WIDE), :] = piece[:, :128]
            field_im[pl.ds(at, 2 * WIDE), :] = piece[:, 128:]

    steps = TILTS // BATCH
    fill(0, rows_a)

    def block(turn, carry):
        fill(2 * turn + 1, rows_b)
        multiply(2 * turn, rows_a)
        fill(jnp.minimum(2 * turn + 2, steps - 1), rows_a)
        multiply(2 * turn + 1, rows_b)
        return carry

    lax.fori_loop(0, steps // 2, block, 0)

    count = GROUP * TILE
    for col in range(WIDE):
        values = jnp.concatenate(
            [
                jnp.concatenate(
                    [ref[pl.ds(col + WIDE * part, TILTS, stride=STEP), :] for part in range(2)], 0
                ).astype(jnp.bfloat16)
                for ref in (field_re, field_im)
            ],
            1,
        )
        mixed = jnp.dot(coef_ref[...], values, preferred_element_type=jnp.float32)
        sums_re[pl.ds(col, count, stride=WIDE), :] = mixed[:count, :count] - mixed[count:, count:]
        sums_im[pl.ds(col, count, stride=WIDE), :] = mixed[count:, :count] + mixed[:count, count:]

    block_of = lax.broadcasted_iota(jnp.int32, (WIDE, 128), 1) // TILE
    for tile in range(GROUP):
        for half in range(2):
            parts = []
            for ref in (sums_re, sums_im):
                total = jnp.zeros((WIDE, 128), jnp.float32)
                for spot in range(8):
                    at = (tile * TILE + half * 8 + spot) * WIDE
                    turned = ref[at : at + WIDE, :]
                    turn = ((spot - tile) * TILE) % 128
                    if turn:
                        turned = pltpu.roll(turned, turn, 1)
                    total = jnp.where(block_of == spot, turned, total)
                parts.append(total)
            parts = [parts[0] * peak_re - parts[1] * peak_im, parts[0] * peak_im + parts[1] * peak_re]
            parts = jnp.concatenate(parts, 0).astype(out_ref.dtype)
            for copy in range(2):
                out_ref[tile + copy * GROUP, :, half * 128 : (half + 1) * 128] = parts


def field_sums(shifts, start, own, mate, own_table, mate_table, back, coef):
    vmem = pl.BlockSpec(memory_space=pltpu.VMEM)
    smem = pl.BlockSpec(memory_space=pltpu.SMEM)
    return pl.pallas_call(
        field_kernel,
        out_shape=jax.ShapeDtypeStruct((2 * GROUP, 2 * WIDE, TILE * TILE), jnp.bfloat16),
        in_specs=[smem, smem] + [vmem] * 6,
        out_specs=vmem,
        scratch_shapes=[
            pltpu.VMEM((4, 2 * ROWS_IN, GRID // 4), jnp.bfloat16),
            pltpu.VMEM((GRID // 128, ROWS_IN, 128), jnp.float32),
            pltpu.VMEM((GRID // 128, ROWS_IN, 128), jnp.float32),
            pltpu.VMEM((2 * WIDE, KU), jnp.bfloat16),
            pltpu.VMEM((BLOCK, KU), jnp.bfloat16),
            pltpu.VMEM((BLOCK, KU), jnp.bfloat16),
            pltpu.VMEM(((TILTS + 1) * STEP, 128), jnp.float32),
            pltpu.VMEM(((TILTS + 1) * STEP, 128), jnp.float32),
            pltpu.VMEM(((GROUP * TILE + 1) * WIDE, 128), jnp.float32),
            pltpu.VMEM(((GROUP * TILE + 1) * WIDE, 128), jnp.float32),
        ],
        compiler_params=pltpu.CompilerParams(vmem_limit_bytes=30 * 1024 * 1024),
    )(
        shifts,
        start,
        own,
        mate,
        own_table,
        mate_table,
        back,
        coef,
    )


def probe_kernel(half_ref, own_ref, mate_ref, high_ref, low_ref, out_ref, turned):
    half = half_ref[0]
    core = half % 2
    spots = TILE * TILE
    index = lax.broadcasted_iota(jnp.int32, (1, 1, WIDE, spots), 2) + (3 * BAND)
    turns = jnp.bitwise_and(index * half, 3)
    cosine = jnp.where(turns == 0, 1.0, jnp.where(turns == 2, -1.0, 0.0))
    sine = jnp.where(turns == 1, 1.0, jnp.where(turns == 3, -1.0, 0.0))
    for ref, place in ((own_ref, core), (mate_ref, 1 - core)):
        sums = ref[...].astype(jnp.float32)
        real, imag = sums[:, :, :WIDE], sums[:, :, WIDE:]
        at = pl.multiple_of(place * PART_ROWS, 128)
        for part, value in enumerate((real * cosine - imag * sine, real * sine + imag * cosine)):
            turned[part * spots : (part + 1) * spots, pl.ds(at, PART_ROWS)] = (
                value.astype(jnp.bfloat16).reshape(PART_ROWS, spots).T
            )
    both = jnp.dot(turned[...], high_ref[...], preferred_element_type=jnp.float32)
    both = both + jnp.dot(turned[...], low_ref[...], preferred_element_type=jnp.float32)
    share = out_ref.shape[1]
    real = both[:spots, :share] - both[spots:, share:]
    imag = both[:spots, share:] + both[spots:, :share]
    out_ref[...] = real * real + imag * imag


def probe_all(half, own, mate, high, low):
    vmem = pl.BlockSpec(memory_space=pltpu.VMEM)
    smem = pl.BlockSpec(memory_space=pltpu.SMEM)
    return pl.pallas_call(
        probe_kernel,
        out_shape=jax.ShapeDtypeStruct((TILE * TILE, GRID // HALVES), jnp.float32),
        in_specs=[smem] + [vmem] * 4,
        out_specs=vmem,
        scratch_shapes=[pltpu.VMEM((2 * TILE * TILE, 2 * PART_ROWS), jnp.bfloat16)],
        compiler_params=pltpu.CompilerParams(vmem_limit_bytes=24 * 1024 * 1024),
    )(half, own, mate, high, low)


def mixing_table(tilt_list, beam_list, beam_table, positions):
    levels = beam_table.shape[0]
    selector = (beam_list[:, None] == jnp.arange(levels, dtype=jnp.int32)[None, :]).astype(
        jnp.float32
    )
    weights = jnp.dot(selector, beam_table, precision=lax.Precision.HIGHEST)
    winding = jnp.bitwise_and(
        positions[:, 0:1] * tilt_list[None, :, 0] + positions[:, 1:2] * tilt_list[None, :, 1],
        GRID - 1,
    )
    coef_angle = two_pi * winding.astype(jnp.float32) / GRID
    cosine = jnp.cos(coef_angle)
    sine_part = jnp.sin(coef_angle)
    coef_re = weights[None, :, 0] * cosine + weights[None, :, 1] * sine_part
    coef_im = weights[None, :, 1] * cosine - weights[None, :, 0] * sine_part
    return jnp.concatenate(
        [jnp.concatenate([coef_re, -coef_im], 1), jnp.concatenate([coef_im, coef_re], 1)], 0
    ).astype(jnp.bfloat16)


def doubled(block, axis, place, strides, size):
    for stride in strides:
        other = lax.ppermute(block, axis, [(i, i ^ stride) for i in range(size)])
        upper = jnp.bitwise_and(place, stride) != 0
        block = jnp.concatenate(
            [jnp.where(upper, other, block), jnp.where(upper, block, other)], 0
        )
    return block


def groups(kind):
    flat = np.arange(64).reshape(4, 2, 2, 4)
    if kind == "depth":
        return flat.reshape(4, 16).T.tolist()
    if kind == "plane":
        return flat.reshape(4, 16).tolist()
    return flat.reshape(8, 8).tolist()


def joint_groups():
    flat = np.arange(256).reshape(2, 2, 8, 8)
    return flat.transpose(2, 1, 0, 3).reshape(16, 16).tolist()


def local(potential, tilt_ids, beam_index, beam_table, positions):
    half = lax.axis_index("half")
    dev = lax.axis_index("dev")
    chip, core = half // 2, half % 2
    rows = potential.shape[0]

    piece = column_piece(potential)
    piece = lax.all_to_all(piece, "dev", 0, 0, tiled=True, axis_index_groups=groups("depth"))
    windows = windows_of(piece.reshape(2 * rows, 2 * CHIP_COLS), positions)
    windows, tilt_ids, beam_index, dev, core_late = lax.optimization_barrier(
        (windows, tilt_ids, beam_index, dev, core)
    )
    group, member = dev // GROUP, dev % GROUP
    info = jnp.concatenate([tilt_ids, beam_index[:, None]], 1)
    tilt_info = doubled(info, "half", half, (1, 2), HALVES)
    columns = lax.all_to_all(
        windows, "dev", 0, 0, tiled=True, axis_index_groups=groups("plane")
    )
    columns, group_late = lax.optimization_barrier((columns, group))
    mate = lax.ppermute(columns, "half", [(i, i ^ 1) for i in range(HALVES)])

    notes = columns[:, : positions.shape[0], 2 * ROWS_IN :].astype(jnp.int32)
    notes = lax.dynamic_slice_in_dim(notes, (group % 2) * GROUP, GROUP, 0)
    notes = notes.reshape(GROUP * positions.shape[0], NOTE)
    spots = notes[:, :2] * 128 + notes[:, 2:]
    coef = mixing_table(tilt_info[:, :2], tilt_info[:, 2], beam_table, spots)

    row_tables = [
        lax.dynamic_index_in_dim(jnp.asarray(row_table()), place, 0, keepdims=False)
        for place in (core_late, 1 - core_late)
    ]
    back = lax.dynamic_index_in_dim(jnp.asarray(back_row_table()), group_late, 0, keepdims=False)
    shifts = (REACH - tilt_info[:, :2]).T + jnp.stack([jnp.int32(0), WIDE * core])[:, None]
    first = WIDE * (chip * 2 * GROUP + member * 2 + core) - BAND
    zero_row = BAND + REACH - 2 * WIDE * (chip * GROUP + member)
    start = jnp.stack([first, core, zero_row]).astype(jnp.int32)
    sums = field_sums(shifts, start, columns, mate, *row_tables, back, coef)

    sums = lax.all_to_all(
        sums,
        ("half", "dev"), 0, 0, tiled=True, axis_index_groups=joint_groups(),
    )
    mates = lax.ppermute(sums, "half", [(i, i ^ 1) for i in range(HALVES)])
    sums, mates = (x.reshape(2, GROUP, 2 * WIDE, TILE * TILE) for x in (sums, mates))

    high, low = (jnp.asarray(t) for t in back_column_table())
    place = half.reshape(1)
    probe = probe_all(place, sums, mates, high, low)
    return probe.reshape(TILE, TILE, GRID // HALVES)


def solution(mesh):
    return jax.shard_map(
        local,
        mesh=mesh,
        in_specs=(P("dev", None), P("half", None), P("half"), P(), P("dev", None)),
        out_specs=P("dev", None, "half"),
        check_vma=False,
    )
```

```python
import functools
import math

import jax
import jax.numpy as jnp
import ml_dtypes
import numpy as np
from jax import lax
from jax.experimental import pallas as pl
from jax.experimental.pallas import tpu as pltpu
from jax.sharding import PartitionSpec as P

two_pi = 2.0 * math.pi
propagation_rate = 0.6

GRID = 1024
TILTS = 256
REACH = 128
BAND = 341
GROUP = 8
HALVES = 4
TILE = 16
WIDE = 24
PARTS = GROUP * HALVES
PART_ROWS = GROUP * 2 * WIDE
ROWS_IN = 2 * WIDE + 2 * REACH
CHIP_COLS = GROUP * 2 * WIDE + 2 * REACH
NOTE = 4
LANES = 2 * ROWS_IN + NOTE
KU = 768
BATCH = 16
BLOCK = 2 * BATCH * WIDE
STEP = 2 * WIDE + 1


def spread_of(row, xnp=np):
    turn = row * 0.6180339887498949
    return xnp.exp2(turn - xnp.floor(turn))


def angles(product):
    return np.mod(product, GRID).astype(np.float64) * (2.0 * np.pi / GRID)


def two_parts(table):
    high = table.astype(np.float32).astype(ml_dtypes.bfloat16)
    low = (table - high.astype(np.float64)).astype(np.float32).astype(ml_dtypes.bfloat16)
    return high, low


@functools.lru_cache(maxsize=None)
def column_table():
    angle = angles(np.arange(GRID)[:, None] * np.arange(128)[None, :])
    return np.stack(two_parts(np.concatenate([np.cos(angle), np.sin(angle)], 1)))


@functools.lru_cache(maxsize=None)
def row_table():
    core, pair, source, depth, inner = np.meshgrid(
        np.arange(2), np.arange(2), np.arange(16), np.arange(4), np.arange(4), indexing="ij"
    )
    inner = 4 * inner + 2 * pair + core
    rows = ((depth * 16 + source) * TILE + inner).reshape(4, GRID // 4)
    angle = angles(rows[:, :, None] * (np.arange(GRID // 4) - BAND - REACH)[None, None, :])
    table = np.stack([np.cos(angle), np.sin(angle)], 2)
    table = table / spread_of(rows % TILE)[:, :, None, None]
    table = table.reshape(2, 2, GRID // 4, 2, 2, 128).transpose(0, 1, 2, 4, 3, 5)
    return table.reshape(2, 2, GRID // 4, 512).astype(np.float32).astype(ml_dtypes.bfloat16)


@functools.lru_cache(maxsize=None)
def back_row_table():
    index = np.arange(KU) - BAND
    result = []
    for group in range(8):
        rows = np.arange(GROUP * TILE) + group * GROUP * TILE
        angle = angles(index[:, None] * rows[None, :])
        angle = angle - (propagation_rate / GRID) * (index * index).astype(np.float64)[:, None]
        cosine, sine = np.cos(angle), np.sin(angle)
        result.append(np.concatenate([cosine, sine], 1))
    return np.stack(result).astype(np.float32).astype(ml_dtypes.bfloat16)


@functools.lru_cache(maxsize=None)
def back_column_table():
    core, chip, member = np.meshgrid(np.arange(2), np.arange(2), np.arange(GROUP), indexing="ij")
    part = (chip * 2 * GROUP + member * 2 + core).reshape(-1)
    index = (part[:, None] * WIDE + np.arange(WIDE)[None, :]).reshape(-1) - BAND
    cols = np.arange(GRID // HALVES)
    angle = angles(index[:, None] * cols[None, :])
    angle = angle - (propagation_rate / GRID) * (index * index).astype(np.float64)[:, None]
    scale = 1.0 / (GRID * GRID)
    return two_parts(np.concatenate([np.cos(angle), np.sin(angle)], 1) * scale)


def chosen(rows, cols, source):
    row = lax.broadcasted_iota(jnp.int32, (rows, cols), 0)
    col = lax.broadcasted_iota(jnp.int32, (rows, cols), 1)
    return jnp.where(col == source(row), 1.0, 0.0).astype(jnp.bfloat16)


def column_kernel(field_ref, table_ref, out_ref, field_in, table, arrived):
    copies = [
        pltpu.make_async_copy(field_ref, field_in, arrived.at[0]),
        pltpu.make_async_copy(table_ref, table, arrived.at[1]),
    ]
    for copy in copies:
        copy.start()
    half = lax.axis_index("half")
    chip, core = half // 2, half % 2
    first = chip * (2 * GROUP * WIDE) - BAND - REACH
    rows = field_in.shape[0] // 2
    pick = chosen(rows, 2 * rows, lambda row: 4 * (row % 4) + 2 * (row // 4) + core)
    row = lax.broadcasted_iota(jnp.int32, (rows, 128), 0)
    spread = spread_of(4 * (row % 4) + 2 * (row // 4) + core, jnp)[:, :1]
    copies[0].wait()
    field = jnp.dot(pick, field_in[...], preferred_element_type=jnp.float32)
    column = lax.broadcasted_iota(jnp.int32, (rows, GRID), 1)
    turn = jnp.bitwise_and(first * column, GRID - 1)
    phase = field - (two_pi / GRID) * turn.astype(jnp.float32)
    cosine, sine = jnp.cos(phase) * spread, jnp.sin(phase) * spread
    waves = [cosine, sine]
    column = column[:, :128]
    for chunk in range(1, CHIP_COLS // 128):
        eighth = jnp.bitwise_and(chunk * column, 7).astype(jnp.float32) * (two_pi / 8)
        turn_re, turn_im = (
            jnp.concatenate([x] * (GRID // 128), 1) for x in (jnp.cos(eighth), jnp.sin(eighth))
        )
        waves += [cosine * turn_re + sine * turn_im, sine * turn_re - cosine * turn_im]
    wave = jnp.concatenate(waves, 0)
    high = wave.astype(jnp.bfloat16)
    low = (wave - high.astype(jnp.float32)).astype(jnp.bfloat16)
    count = wave.shape[0]
    copies[1].wait()
    both = jnp.dot(jnp.concatenate([high, low], 0), table[0], preferred_element_type=jnp.float32)
    mixed = both[:count] + both[count:]
    mixed = mixed + jnp.dot(high, table[1], preferred_element_type=jnp.float32)
    cols_re, cols_im = [], []
    for chunk in range(CHIP_COLS // 128):
        cosine = mixed[2 * rows * chunk : 2 * rows * chunk + rows]
        sine = mixed[2 * rows * chunk + rows : 2 * rows * (chunk + 1)]
        cols_re.append(cosine[:, :128] + sine[:, 128:])
        cols_im.append(sine[:, :128] - cosine[:, 128:])
    piece = jnp.concatenate(cols_re + cols_im, 1).astype(jnp.bfloat16)
    for copy in range(out_ref.shape[0]):
        out_ref[copy] = piece


def column_piece(potential):
    vmem = pl.BlockSpec(memory_space=pltpu.VMEM)
    table = column_table()
    rows = potential.shape[0]
    anywhere = pl.BlockSpec(memory_space=pltpu.HBM)
    return pl.pallas_call(
        column_kernel,
        out_shape=jax.ShapeDtypeStruct((4, rows // 2, 2 * CHIP_COLS), jnp.bfloat16),
        in_specs=[anywhere, anywhere],
        out_specs=vmem,
        scratch_shapes=[
            pltpu.VMEM(potential.shape, jnp.bfloat16),
            pltpu.VMEM(table.shape, jnp.bfloat16),
            pltpu.SemaphoreType.DMA((2,)),
        ],
        compiler_params=pltpu.CompilerParams(vmem_limit_bytes=56 * 1024 * 1024),
    )(potential, jnp.asarray(table))


def window_kernel(piece_ref, spot_ref, out_ref):
    rows = piece_ref.shape[0]
    pick = chosen(rows, rows, lambda row: 8 * ((row // 4) % 4) + 4 * (row // 16) + row % 4)
    piece = jnp.dot(pick, piece_ref[...], preferred_element_type=jnp.float32)
    spots = spot_ref[...]
    note = jnp.concatenate([spots >> 7, jnp.bitwise_and(spots, 127)], 1).astype(jnp.float32)
    note = jnp.concatenate([note, jnp.zeros_like(note)], 0)
    for member in range(GROUP):
        at = 2 * WIDE * member
        window = jnp.concatenate(
            [piece[:, part * CHIP_COLS + at : part * CHIP_COLS + at + ROWS_IN] for part in range(2)]
            + [note],
            1,
        ).astype(jnp.bfloat16)
        for copy in range(2):
            out_ref[member + copy * GROUP] = window


def windows_of(piece, spots):
    vmem = pl.BlockSpec(memory_space=pltpu.VMEM)
    return pl.pallas_call(
        window_kernel,
        out_shape=jax.ShapeDtypeStruct((2 * GROUP, piece.shape[0], LANES), jnp.bfloat16),
        in_specs=[vmem, vmem],
        out_specs=vmem,
        compiler_params=pltpu.CompilerParams(vmem_limit_bytes=16 * 1024 * 1024),
    )(piece, spots)


def field_kernel(
    shift_ref,
    start_ref,
    own_ref,
    mate_ref,
    own_table,
    mate_table,
    back_ref,
    coef_ref,
    out_ref,
    turned_ref,
    spec_re,
    spec_im,
    mask,
    rows_a,
    rows_b,
    field_re,
    field_im,
    sums_re,
    sums_im,
):
    first_core = start_ref[1] == 0
    for pair in range(2):
        for place, ref in enumerate((own_ref, mate_ref)):
            block = ref[:, 16 * pair : 16 * pair + 16, :]
            block = block.reshape(GRID // 4, LANES)[:, : 2 * ROWS_IN]
            turned_ref[2 * place + pair] = block.T
    for part in range(2):
        lanes = slice(256 * part, 256 * (part + 1))
        each = []
        for place, ref in enumerate((own_table, mate_table)):
            for pair in range(2):
                both = jnp.dot(
                    turned_ref[2 * place + pair],
                    ref[pair, :, lanes],
                    preferred_element_type=jnp.float32,
                )
                each.append(
                    (
                        both[:ROWS_IN, :128] + both[ROWS_IN:, 128:],
                        both[ROWS_IN:, :128] - both[:ROWS_IN, 128:],
                    )
                )
        each = [
            tuple(jnp.where(first_core, x, y) for x, y in zip(each[one], each[two]))
            for one, two in ((0, 2), (2, 0), (1, 3), (3, 1))
        ]
        (re0, im0), (re1, im1), (re2, im2), (re3, im3) = each
        even, even_less = (re0 + re2, im0 + im2), (re0 - re2, im0 - im2)
        odd, odd_less = (re1 + re3, im1 + im3), (im1 - im3, re3 - re1)
        for quarter, left, right, sign in (
            (0, even, odd, 1),
            (1, even_less, odd_less, 1),
            (2, even, odd, -1),
            (3, even_less, odd_less, -1),
        ):
            for ref, x, y in ((spec_re, left[0], right[0]), (spec_im, left[1], right[1])):
                ref[2 * quarter + part] = x + y if sign > 0 else x - y

    peak_row = start_ref[2]
    peak_at = jnp.clip(peak_row, 0, ROWS_IN - 1)
    peak_lane = BAND + REACH
    peak_re, peak_im = (
        ref[peak_lane // 128, pl.ds(peak_at, 1), :][:, peak_lane % 128 : peak_lane % 128 + 1]
        for ref in (spec_re, spec_im)
    )
    power = peak_re * peak_re + peak_im * peak_im
    held = jnp.logical_and(power > 1e-6, peak_row == peak_at)
    peak_re = jnp.where(held, peak_re, 1.0)
    peak_im = jnp.where(held, peak_im, 0.0)
    inverse = 1.0 / jnp.where(held, power, 1.0)
    scale_re, scale_im = peak_re * inverse, -peak_im * inverse
    for chunk in range(GRID // 128):
        value_re, value_im = spec_re[chunk], spec_im[chunk]
        spec_re[chunk] = value_re * scale_re - value_im * scale_im
        spec_im[chunk] = value_re * scale_im + value_im * scale_re

    first = start_ref[0]
    row_index = lax.broadcasted_iota(jnp.int32, (WIDE, KU), 0) + first
    lane_index = lax.broadcasted_iota(jnp.int32, (WIDE, KU), 1) - BAND
    inside = 9 * (row_index * row_index + lane_index * lane_index) < GRID * GRID
    inside = jnp.where(inside, 1.0, 0.0)
    mask[...] = jnp.concatenate([inside, inside], 0).astype(jnp.bfloat16)
    chunks = KU // 128

    def shifted(tilt, rows, at):
        row_at = shift_ref[1, tilt]
        lane_at = shift_ref[0, tilt]
        base = jnp.where(lane_at >= 128, 1, 0)
        rest = lane_at - 128 * base
        lanes = lax.broadcasted_iota(jnp.int32, (2 * WIDE, 128), 1)
        keep = lanes < 128 - rest
        turn = jnp.bitwise_and(128 - rest, 127)
        before = None
        for chunk in range(chunks + 1):
            window = jnp.concatenate(
                [ref[base + chunk, pl.ds(row_at, WIDE), :] for ref in (spec_re, spec_im)], 0
            )
            rolled = pltpu.roll(window.astype(jnp.bfloat16), turn, 1)
            if chunk:
                lanes_at = (chunk - 1) * 128
                rows[at : at + 2 * WIDE, lanes_at : lanes_at + 128] = (
                    jnp.where(keep, before, rolled) * mask[:, lanes_at : lanes_at + 128]
                )
            before = rolled

    def fill(step, rows):
        for spot in range(BATCH):
            shifted(step * BATCH + spot, rows, spot * 2 * WIDE)

    def multiply(step, rows):
        result = jnp.dot(rows[...], back_ref[...], preferred_element_type=jnp.float32)
        for spot in range(BATCH):
            at = step * BATCH * STEP + spot * STEP
            piece = result[spot * 2 * WIDE : (spot + 1) * 2 * WIDE]
            field_re[pl.ds(at, 2 * WIDE), :] = piece[:, :128]
            field_im[pl.ds(at, 2 * WIDE), :] = piece[:, 128:]

    steps = TILTS // BATCH
    fill(0, rows_a)

    def block(turn, carry):
        fill(2 * turn + 1, rows_b)
        multiply(2 * turn, rows_a)
        fill(2 * turn + 2, rows_a)
        multiply(2 * turn + 1, rows_b)
        return carry

    lax.fori_loop(0, steps // 2 - 1, block, 0)
    fill(steps - 1, rows_b)
    multiply(steps - 2, rows_a)
    multiply(steps - 1, rows_b)

    count = GROUP * TILE
    for col in range(WIDE):
        values = jnp.concatenate(
            [
                jnp.concatenate(
                    [ref[pl.ds(col + WIDE * part, TILTS, stride=STEP), :] for part in range(2)], 0
                ).astype(jnp.bfloat16)
                for ref in (field_re, field_im)
            ],
            1,
        )
        mixed = jnp.dot(coef_ref[...], values, preferred_element_type=jnp.float32)
        sums_re[pl.ds(col, count, stride=WIDE), :] = mixed[:count, :count] - mixed[count:, count:]
        sums_im[pl.ds(col, count, stride=WIDE), :] = mixed[count:, :count] + mixed[:count, count:]

    block_of = lax.broadcasted_iota(jnp.int32, (WIDE, 128), 1) // TILE
    for tile in range(GROUP):
        for half in range(2):
            parts = []
            for ref in (sums_re, sums_im):
                total = jnp.zeros((WIDE, 128), jnp.float32)
                for spot in range(8):
                    at = (tile * TILE + half * 8 + spot) * WIDE
                    turned = ref[at : at + WIDE, :]
                    turn = ((spot - tile) * TILE) % 128
                    if turn:
                        turned = pltpu.roll(turned, turn, 1)
                    total = jnp.where(block_of == spot, turned, total)
                parts.append(total)
            parts = [parts[0] * peak_re - parts[1] * peak_im, parts[0] * peak_im + parts[1] * peak_re]
            parts = jnp.concatenate(parts, 0).astype(out_ref.dtype)
            for copy in range(2):
                out_ref[tile + copy * GROUP, :, half * 128 : (half + 1) * 128] = parts


def field_sums(shifts, start, own, mate, own_table, mate_table, back, coef):
    vmem = pl.BlockSpec(memory_space=pltpu.VMEM)
    smem = pl.BlockSpec(memory_space=pltpu.SMEM)
    return pl.pallas_call(
        field_kernel,
        out_shape=jax.ShapeDtypeStruct((2 * GROUP, 2 * WIDE, TILE * TILE), jnp.bfloat16),
        in_specs=[smem, smem] + [vmem] * 6,
        out_specs=vmem,
        scratch_shapes=[
            pltpu.VMEM((4, 2 * ROWS_IN, GRID // 4), jnp.bfloat16),
            pltpu.VMEM((GRID // 128, ROWS_IN, 128), jnp.float32),
            pltpu.VMEM((GRID // 128, ROWS_IN, 128), jnp.float32),
            pltpu.VMEM((2 * WIDE, KU), jnp.bfloat16),
            pltpu.VMEM((BLOCK, KU), jnp.bfloat16),
            pltpu.VMEM((BLOCK, KU), jnp.bfloat16),
            pltpu.VMEM(((TILTS + 1) * STEP, 128), jnp.float32),
            pltpu.VMEM(((TILTS + 1) * STEP, 128), jnp.float32),
            pltpu.VMEM(((GROUP * TILE + 1) * WIDE, 128), jnp.float32),
            pltpu.VMEM(((GROUP * TILE + 1) * WIDE, 128), jnp.float32),
        ],
        compiler_params=pltpu.CompilerParams(vmem_limit_bytes=30 * 1024 * 1024),
    )(
        shifts,
        start,
        own,
        mate,
        own_table,
        mate_table,
        back,
        coef,
    )


def probe_kernel(half_ref, own_ref, mate_ref, high_ref, low_ref, out_ref, turned):
    half = half_ref[0]
    core = half % 2
    spots = TILE * TILE
    index = lax.broadcasted_iota(jnp.int32, (1, 1, WIDE, spots), 2) + (3 * BAND)
    turns = jnp.bitwise_and(index * half, 3)
    cosine = jnp.where(turns == 0, 1.0, jnp.where(turns == 2, -1.0, 0.0))
    sine = jnp.where(turns == 1, 1.0, jnp.where(turns == 3, -1.0, 0.0))
    for ref, place in ((own_ref, core), (mate_ref, 1 - core)):
        sums = ref[...].astype(jnp.float32)
        real, imag = sums[:, :, :WIDE], sums[:, :, WIDE:]
        at = pl.multiple_of(place * PART_ROWS, 128)
        for part, value in enumerate((real * cosine - imag * sine, real * sine + imag * cosine)):
            turned[part * spots : (part + 1) * spots, pl.ds(at, PART_ROWS)] = (
                value.astype(jnp.bfloat16).reshape(PART_ROWS, spots).T
            )
    both = jnp.dot(turned[...], high_ref[...], preferred_element_type=jnp.float32)
    both = both + jnp.dot(turned[...], low_ref[...], preferred_element_type=jnp.float32)
    share = out_ref.shape[1]
    real = both[:spots, :share] - both[spots:, share:]
    imag = both[:spots, share:] + both[spots:, :share]
    out_ref[...] = real * real + imag * imag


def probe_all(half, own, mate, high, low):
    vmem = pl.BlockSpec(memory_space=pltpu.VMEM)
    smem = pl.BlockSpec(memory_space=pltpu.SMEM)
    return pl.pallas_call(
        probe_kernel,
        out_shape=jax.ShapeDtypeStruct((TILE * TILE, GRID // HALVES), jnp.float32),
        in_specs=[smem] + [vmem] * 4,
        out_specs=vmem,
        scratch_shapes=[pltpu.VMEM((2 * TILE * TILE, 2 * PART_ROWS), jnp.bfloat16)],
        compiler_params=pltpu.CompilerParams(vmem_limit_bytes=24 * 1024 * 1024),
    )(half, own, mate, high, low)


def mixing_table(tilt_list, beam_list, beam_table, positions):
    levels = beam_table.shape[0]
    selector = (beam_list[:, None] == jnp.arange(levels, dtype=jnp.int32)[None, :]).astype(
        jnp.float32
    )
    weights = jnp.dot(selector, beam_table, precision=lax.Precision.HIGHEST)
    winding = jnp.bitwise_and(
        positions[:, 0:1] * tilt_list[None, :, 0] + positions[:, 1:2] * tilt_list[None, :, 1],
        GRID - 1,
    )
    coef_angle = two_pi * winding.astype(jnp.float32) / GRID
    cosine = jnp.cos(coef_angle)
    sine_part = jnp.sin(coef_angle)
    coef_re = weights[None, :, 0] * cosine + weights[None, :, 1] * sine_part
    coef_im = weights[None, :, 1] * cosine - weights[None, :, 0] * sine_part
    return jnp.concatenate(
        [jnp.concatenate([coef_re, -coef_im], 1), jnp.concatenate([coef_im, coef_re], 1)], 0
    ).astype(jnp.bfloat16)


def doubled(block, axis, place, strides, size):
    for stride in strides:
        other = lax.ppermute(block, axis, [(i, i ^ stride) for i in range(size)])
        upper = jnp.bitwise_and(place, stride) != 0
        block = jnp.concatenate(
            [jnp.where(upper, other, block), jnp.where(upper, block, other)], 0
        )
    return block


def groups(kind):
    flat = np.arange(64).reshape(4, 2, 2, 4)
    if kind == "depth":
        return flat.reshape(4, 16).T.tolist()
    if kind == "plane":
        return flat.reshape(4, 16).tolist()
    return flat.reshape(8, 8).tolist()


def joint_groups():
    flat = np.arange(256).reshape(2, 2, 8, 8)
    return flat.transpose(2, 1, 0, 3).reshape(16, 16).tolist()


def local(potential, tilt_ids, beam_index, beam_table, positions):
    half = lax.axis_index("half")
    dev = lax.axis_index("dev")
    chip, core = half // 2, half % 2
    rows = potential.shape[0]

    piece = column_piece(potential)
    piece = lax.all_to_all(piece, "dev", 0, 0, tiled=True, axis_index_groups=groups("depth"))
    windows = windows_of(piece.reshape(2 * rows, 2 * CHIP_COLS), positions)
    windows, tilt_ids, beam_index, dev, core_late = lax.optimization_barrier(
        (windows, tilt_ids, beam_index, dev, core)
    )
    group, member = dev // GROUP, dev % GROUP
    info = jnp.concatenate([tilt_ids, beam_index[:, None]], 1)
    tilt_info = doubled(info, "half", half, (1, 2), HALVES)
    columns = lax.all_to_all(
        windows, "dev", 0, 0, tiled=True, axis_index_groups=groups("plane")
    )
    columns, group_late = lax.optimization_barrier((columns, group))
    mate = lax.ppermute(columns, "half", [(i, i ^ 1) for i in range(HALVES)])

    notes = columns[:, : positions.shape[0], 2 * ROWS_IN :].astype(jnp.int32)
    notes = lax.dynamic_slice_in_dim(notes, (group % 2) * GROUP, GROUP, 0)
    notes = notes.reshape(GROUP * positions.shape[0], NOTE)
    spots = notes[:, :2] * 128 + notes[:, 2:]
    coef = mixing_table(tilt_info[:, :2], tilt_info[:, 2], beam_table, spots)

    row_tables = [
        lax.dynamic_index_in_dim(jnp.asarray(row_table()), place, 0, keepdims=False)
        for place in (core_late, 1 - core_late)
    ]
    back = lax.dynamic_index_in_dim(jnp.asarray(back_row_table()), group_late, 0, keepdims=False)
    shifts = (REACH - tilt_info[:, :2]).T + jnp.stack([jnp.int32(0), WIDE * core])[:, None]
    first = WIDE * (chip * 2 * GROUP + member * 2 + core) - BAND
    zero_row = BAND + REACH - 2 * WIDE * (chip * GROUP + member)
    start = jnp.stack([first, core, zero_row]).astype(jnp.int32)
    sums = field_sums(shifts, start, columns, mate, *row_tables, back, coef)

    sums = lax.all_to_all(
        sums,
        ("half", "dev"), 0, 0, tiled=True, axis_index_groups=joint_groups(),
    )
    mates = lax.ppermute(sums, "half", [(i, i ^ 1) for i in range(HALVES)])
    sums, mates = (x.reshape(2, GROUP, 2 * WIDE, TILE * TILE) for x in (sums, mates))

    high, low = (jnp.asarray(t) for t in back_column_table())
    place = half.reshape(1)
    probe = probe_all(place, sums, mates, high, low)
    return probe.reshape(TILE, TILE, GRID // HALVES)


def solution(mesh):
    return jax.shard_map(
        local,
        mesh=mesh,
        in_specs=(P("dev", None), P("half", None), P("half"), P(), P("dev", None)),
        out_specs=P("dev", None, "half"),
        check_vma=False,
    )
```
